512 devices in a mesh: ctx: 32 (over z, core), inner: 16 (over y, x).
Axes of the slice: x: 4, y: 4, z: 16, core: 2. Of those that a mesh axis runs over, the one named last changes fastest.
Arguments:
- tokens: bfloat16 [65536, 2048], P(('ctx', 'inner')), may hold values from -6 to 6
- project_weight: bfloat16 [2048, 2, 4096], P('ctx', None, 'inner'), may hold values from -0.125 to 0.125
- state_weight: bfloat16 [2048, 2, 512], P('ctx', None, 'inner'), may hold values from -0.125 to 0.125
- step_weight: bfloat16 [2048, 64], P('ctx', 'inner'), may hold values from -0.125 to 0.125
- mixer_taps: float32 [5, 4096], P(None, 'inner'), may hold values from -2.5 to 2.5
- state_taps: float32 [5, 2, 512], replicated, may hold values from -2.5 to 2.5
- step_bias: float32 [64], P('inner'), may hold values from -4.6 to -2.3
- decay_log: float32 [64], P('inner'), may hold values from -13 to 0.5, as said below
- norm_gain: float32 [4096], replicated, may hold values from 0.1 to 1.9
Outputs:
- mixed_output: bfloat16 [65536, 4096], P(('ctx', 'inner'))
The draws below stay inside these ranges and needn't reach their ends.
Inputs may be any that keep to these rules, and one draw needn't show every extreme that they name: `decay_log`: one value a head.
All inputs are finite; a program needn't handle non-finite values.
Results may differ from the reference program's by a relative error of at most 0.0075.
Values may be sent and summed in bfloat16 or wider, within the bound.
A program may use at most 64 MiB of HBM per device.

```python
import jax
import jax.numpy as jnp
from jax import lax

D = 2048
H = 64
P_SIZE = 64
N = 128
G = 4
CONV = 4
SPAN = 128
E = 4096
TOKENS = 65536


def draw_decay_log(key, part):
    first_key = jax.random.fold_in(key, 0)
    return jax.random.uniform(first_key, (H,), jnp.float32, -13.0, 0.5)


def block_scale(key, extent, cuts, least, high):
    gain = 1.0
    for position, shards_of in cuts:
        draws = jax.random.uniform(jax.random.fold_in(jax.random.fold_in(key, 6), position), (shards_of,), jnp.float32, least / len(cuts), high / len(cuts))
        gain = gain * jnp.repeat(jnp.exp(draws), extent[position] // shards_of).reshape((-1,) + (1,) * (len(extent) - 1 - position))
    return gain


def noise(rng, shape, scale, most, cuts=(), held_as=jnp.bfloat16):
    factor_of = block_scale(rng, shape, cuts, -0.22, 0.18) if cuts else 1.0
    entries = jax.random.normal(rng, shape, jnp.float32) * scale * factor_of
    return jnp.minimum(jnp.maximum(entries, -most), most).astype(held_as)


def setup_inputs(seed: int = 0) -> dict:
    key_list = jax.random.split(jax.random.key(seed), 10)
    tokens = noise(key_list[0], (TOKENS, D), 1.0, 6.0, ((0, 512),))
    project_weight = noise(key_list[1], (D, 2, E), D ** -0.5, 0.125, ((0, 32), (2, 16)))
    state_weight = noise(key_list[2], (D, 2, G * N), D ** -0.5, 0.125, ((0, 32), (2, 16)))
    step_weight = noise(key_list[3], (D, H), D ** -0.5, 0.125, ((0, 32), (1, 16)))
    mixer_taps = noise(key_list[4], (CONV + 1, E), 0.5, 2.5, ((1, 16),), jnp.float32)
    state_taps = noise(key_list[5], (CONV + 1, 2, G * N), 0.5, 2.5, (), jnp.float32)
    step_bias = jnp.clip(-4.6 + 2.3 * jax.random.uniform(key_list[6], (H,), jnp.float32) ** block_scale(key_list[6], (H,), ((0, 16),), -0.2, 0.2), -4.6, -2.3)
    decay_log = draw_decay_log(jax.random.fold_in(key_list[9], 71), 0)
    norm_gain = jnp.clip(1.0 + 0.18 * jax.random.normal(key_list[8], (E,), jnp.float32), 0.1, 1.9)
    return dict(tokens=tokens, project_weight=project_weight, state_weight=state_weight, step_weight=step_weight, mixer_taps=mixer_taps, state_taps=state_taps, step_bias=step_bias, decay_log=decay_log, norm_gain=norm_gain)


EPSILON = 1e-05

def reference(tokens, project_weight, state_weight, step_weight, mixer_taps, state_taps, step_bias, decay_log, norm_gain):
    length_all = tokens.shape[0]
    blocks = length_all // SPAN
    channels = H * P_SIZE
    group_cols = G * N
    heads_group = H // G
    flat_project = project_weight.reshape(D, 2 * channels)
    flat_state = state_weight.reshape(D, 2 * group_cols)
    taps_all = jnp.concatenate([mixer_taps, state_taps.reshape(CONV + 1, 2 * group_cols)], axis=1)
    rates = -jnp.exp(decay_log)
    lower = jnp.tril(jnp.ones((SPAN, SPAN), dtype=bool))

    def advance(carry, rows):
        state, rim_rows = carry
        projected = jnp.dot(rows, flat_project, preferred_element_type=jnp.float32).astype(jnp.bfloat16)
        state_pre = jnp.dot(rows, flat_state, preferred_element_type=jnp.float32).astype(jnp.bfloat16)
        step_raw = jnp.dot(rows, step_weight, preferred_element_type=jnp.float32).astype(jnp.bfloat16)
        gate_values = projected[:, :channels]
        current = jnp.concatenate([projected[:, channels:], state_pre], axis=1)
        extended = jnp.concatenate([rim_rows, current], axis=0)
        mixed = jnp.broadcast_to(taps_all[CONV], current.shape).astype(jnp.float32)
        for offset in range(CONV):
            mixed = mixed + taps_all[offset] * extended[offset:offset + SPAN].astype(jnp.float32)
        active = jax.nn.silu(mixed).astype(jnp.bfloat16)
        x_vals = active[:, :channels].reshape(SPAN, H, P_SIZE).astype(jnp.float32)
        b_vals = active[:, channels:channels + group_cols].reshape(SPAN, N, G).transpose(0, 2, 1).astype(jnp.float32)
        c_vals = active[:, channels + group_cols:].reshape(SPAN, N, G).transpose(0, 2, 1).astype(jnp.float32)
        step_size = jax.nn.softplus(step_raw.astype(jnp.float32) + step_bias)
        cumul = jnp.cumsum(step_size * rates, axis=0)
        scores = jnp.einsum('tgn,sgn->gts', c_vals, b_vals, precision=lax.Precision.HIGHEST)
        scores = jnp.repeat(scores, heads_group, axis=0)
        cumul_heads = cumul.T
        spacing = jnp.where(lower[None], cumul_heads[:, :, None] - cumul_heads[:, None, :], -jnp.inf)
        mixing = (scores * jnp.exp(spacing) * step_size.T[:, None, :]).astype(jnp.bfloat16)
        diagonal = jnp.einsum('hts,shp->thp', mixing.astype(jnp.float32), x_vals, precision=lax.Precision.HIGHEST)
        ending = cumul[-1]
        to_end = jnp.exp(ending[None] - cumul) * step_size
        b_heads = jnp.repeat(b_vals, heads_group, axis=1)
        weighted_b = lax.optimization_barrier((b_heads * to_end[:, :, None]).astype(jnp.bfloat16)).astype(jnp.float32)
        c_heads = jnp.repeat(c_vals, heads_group, axis=1) * jnp.exp(cumul)[:, :, None]
        weighted_c = lax.optimization_barrier(c_heads.astype(jnp.bfloat16)).astype(jnp.float32)
        fresh = jnp.einsum('shn,shp->hnp', weighted_b, x_vals, precision=lax.Precision.HIGHEST)
        offdiag = jnp.einsum('thn,hnp->thp', weighted_c, state, precision=lax.Precision.HIGHEST)
        state_next = jnp.exp(ending)[:, None, None] * state + fresh
        outputs = (diagonal + offdiag).reshape(SPAN, channels)
        gated = (outputs * jax.nn.silu(gate_values.astype(jnp.float32))).astype(jnp.bfloat16)
        grouped = gated.astype(jnp.float32).reshape(SPAN, G, channels // G)
        power = lax.optimization_barrier(jnp.mean(grouped * grouped, axis=-1, keepdims=True))
        normed = (grouped * lax.rsqrt(power + EPSILON)).reshape(SPAN, channels) * norm_gain
        return ((state_next, extended[SPAN:]), normed.astype(jnp.bfloat16))
    start_carry = (jnp.zeros((H, N, P_SIZE), jnp.float32), jnp.zeros((CONV - 1, channels + 2 * group_cols), jnp.bfloat16))
    _, results = lax.scan(advance, start_carry, tokens.reshape(blocks, SPAN, D))
    return results.reshape(length_all, channels)
```

```python
import functools

import jax
import jax.numpy as jnp
from jax import lax
from jax.experimental import pallas as pl
from jax.experimental.pallas import tpu as pltpu
from jax.sharding import PartitionSpec as P

H = 64
P_SIZE = 64
N = 128
G = 4
CONV = 4
SPAN = 128
EPSILON = 1e-05
MESH = pl.DeviceIdType.MESH
CTX = 32
INNER = 16
SIDE = 4
QUARTERS = 4
VMEM_LIMIT = 60 * 1024 * 1024


def remote(src, dst, send_sem, recv_sem, device):
    return pltpu.make_async_remote_copy(
        src_ref=src,
        dst_ref=dst,
        send_sem=send_sem,
        recv_sem=recv_sem,
        device_id=device,
        device_id_type=MESH,
    )


def landed(ref, sem):
    pltpu.make_async_copy(ref, ref, sem).wait()


def gather_kernel(
    tok_ref,
    project_ref,
    state_ref,
    step_ref,
    out_ref,
    tokens,
    w_project,
    w_rest,
    parts,
    tok_send,
    tok_recv,
    wp_send,
    wp_recv,
    wr_send,
    wr_recv,
    part_send,
    part_recv,
):
    ctx = lax.axis_index("ctx")
    inner = lax.axis_index("inner")
    y, x = inner // SIDE, inner % SIDE
    rows_here = project_ref.shape[0]
    other = ctx + 1 - 2 * (ctx % 2)
    up, down = (ctx + 2) % CTX, (ctx + CTX - 2) % CTX

    def at(dy, dx):
        return ((y + dy) % SIDE) * SIDE + (x + dx) % SIDE

    barrier = pltpu.get_barrier_semaphore()

    def greet(step, carry):
        pl.semaphore_signal(
            barrier, inc=1, device_id={"inner": (inner + step) % INNER}, device_id_type=MESH
        )
        return carry

    lax.fori_loop(1, INNER, greet, 0)
    for peer in (up, down, other):
        pl.semaphore_signal(barrier, inc=1, device_id={"ctx": peer}, device_id_type=MESH)
    pl.semaphore_wait(barrier, INNER - 1 + 3)

    def part_copy(step):
        to = (inner + step) % INNER
        return remote(
            state_ref.at[to // (INNER // G)],
            parts.at[inner],
            part_send,
            part_recv,
            {"inner": to},
        )

    def send_part(step, carry):
        part_copy(step).start()
        return carry

    lax.fori_loop(1, INNER, send_part, 0)
    parts[inner] = state_ref[inner // (INNER // G)]

    def rows_of(place):
        return pl.ds(pl.multiple_of(place * rows_here, rows_here), rows_here)

    def wp_copy(place, to):
        return remote(
            w_project.at[rows_of(place)],
            w_project.at[rows_of(place)],
            wp_send,
            wp_recv.at[place],
            {"ctx": to},
        )

    def wr_copy(place, to):
        return remote(
            w_rest.at[rows_of(place)],
            w_rest.at[rows_of(place)],
            wr_send,
            wr_recv.at[place],
            {"ctx": to},
        )

    w_project[rows_of(ctx)] = project_ref[...]
    for peer in (up, down, other):
        wp_copy(ctx, peer).start()

    quarter = tok_ref.shape[0] // QUARTERS

    def tok_send_to(q, held, move):
        rows = pl.ds(q * quarter, quarter)
        (dy, dx), (ay, ax) = held, move
        slot = ((dy - ay) % SIDE) * SIDE + (dx - ax) % SIDE
        mine = (dy % SIDE) * SIDE + dx % SIDE
        source = tok_ref.at[rows] if mine == 0 else tokens.at[mine, rows]
        remote(
            source,
            tokens.at[slot, rows],
            tok_send,
            tok_recv.at[q * INNER + slot],
            {"inner": at(ay, ax)},
        ).start()

    def tok_wait(q, held):
        slot = (held[0] % SIDE) * SIDE + held[1] % SIDE
        landed(tokens.at[slot, pl.ds(q * quarter, quarter)], tok_recv.at[q * INNER + slot])

    def turn(q, along, across):
        return (across, along) if q < 2 else (along, across)

    def sense(q):
        return 1 if q % 2 == 0 else -1

    for first in (True, False):
        for q in range(QUARTERS):
            for d in (sense(q), -sense(q)):
                tok_send_to(q, (0, 0), turn(q, d, 0) if first else turn(q, 0, d))
    tokens[0] = tok_ref[...]

    landed(parts.at[pl.ds(0, INNER - 1)], part_recv)
    width = 2 * N
    source_row = lax.broadcasted_iota(jnp.int32, (width, width), 0)
    target = lax.broadcasted_iota(jnp.int32, (width, width), 1)
    piece = N // INNER
    goes = (
        ((source_row // piece) % 2) * N + (source_row // (2 * piece)) * piece + source_row % piece
    )
    place = jnp.where(goes == target, 1.0, 0.0).astype(jnp.bfloat16)
    state_cols = lax.dot_general(
        parts[...].reshape(width, rows_here),
        place,
        (((0,), (0,)), ((), ())),
        preferred_element_type=jnp.float32,
    ).astype(jnp.bfloat16)
    w_rest[rows_of(ctx), :width] = state_cols
    w_rest[rows_of(ctx), width:] = step_ref[...]
    for peer in (up, down, other):
        wr_copy(ctx, peer).start()

    def relay(copy, recv, ref, hop):
        behind, ahead = (ctx + CTX - 2 * hop) % CTX, (ctx + 2 * hop) % CTX
        landed(ref.at[rows_of(behind)], recv.at[behind])
        if hop < CTX // 4:
            copy(behind, up).start()
        copy(behind, other).start()
        if hop < CTX // 4:
            landed(ref.at[rows_of(ahead)], recv.at[ahead])
            if hop < CTX // 4 - 1:
                copy(ahead, down).start()
            copy(ahead, other).start()

    def w_relay(hop):
        relay(wp_copy, wp_recv, w_project, hop)
        relay(wr_copy, wr_recv, w_rest, hop)

    def arrive(q, along, across):
        d = sense(q)
        held = turn(q, along, across)
        tok_wait(q, held)
        if across == 0:
            if along == -d:
                tok_send_to(q, held, turn(q, d, 0))
            for e in (d, -d):
                tok_send_to(q, held, turn(q, 0, e))
        elif across == -d:
            tok_send_to(q, held, turn(q, 0, d))

    for q in range(QUARTERS):
        arrive(q, -sense(q), 0)
        arrive(q, sense(q), 0)
        if q % 2:
            w_relay(1 + q // 2)
    for q in range(QUARTERS):
        arrive(q, 2, 0)
        arrive(q, 0, -sense(q))
        if q % 2:
            w_relay(3 + q // 2)
    for step in (-1, 1):
        for q in range(QUARTERS):
            arrive(q, step * sense(q), -sense(q))
        w_relay(5 + (step + 1) // 2)
    for q in range(QUARTERS):
        arrive(q, 2, -sense(q))
    w_relay(7)
    w_relay(8)

    def handed(hop, carry):
        src = (other + 2 * hop) % CTX
        landed(w_project.at[rows_of(src)], wp_recv.at[src])
        landed(w_rest.at[rows_of(src)], wr_recv.at[src])
        return carry

    lax.fori_loop(0, CTX // 2, handed, 0)

    rest_width = w_rest.shape[1]
    project_width = w_project.shape[1]
    span = tok_ref.shape[0]
    done = set()
    for q in range(QUARTERS):
        for along, across in ((-1, 0), (1, 0), (2, 0)):
            done.add((q,) + tuple(v % SIDE for v in turn(q, along, across)))
        for along in range(SIDE):
            done.add((q,) + tuple(v % SIDE for v in turn(q, along, -sense(q))))
    for dy in (0, 1, 3, 2):
        for dx in range(SIDE):
            for q in range(QUARTERS):
                if (dy, dx) != (0, 0) and (q, dy, dx) not in done:
                    tok_wait(q, (dy, dx))

        def multiply(pair, carry, dy=dy):
            first = dy * SIDE + 2 * pair
            rows = tokens[pl.ds(first, 2)].reshape(2 * span, tokens.shape[2])
            wide = jnp.dot(rows, w_project[...], preferred_element_type=jnp.float32).astype(
                jnp.bfloat16
            )
            rest = jnp.dot(rows, w_rest[...], preferred_element_type=jnp.float32).astype(
                jnp.bfloat16
            )
            for half in range(2):
                src = at(dy, 2 * pair + half)
                to = pl.ds(pl.multiple_of(src * span, span), span)
                out_ref[to, :project_width] = wide[half * span : (half + 1) * span]
                out_ref[to, project_width:] = rest[half * span : (half + 1) * span]
            return carry

        lax.fori_loop(0, 2, multiply, 0)

    landed(tokens.at[pl.ds(0, INNER - 1)], tok_send)
    landed(parts.at[pl.ds(0, INNER - 1)], part_send)
    sent = rows_here * (2 + 1 + 7 + 6 + 15)
    landed(w_project.at[pl.ds(0, sent)], wp_send)
    landed(w_rest.at[pl.ds(0, sent)], wr_send)


def gather_project(tokens, project, state, step):
    span, model = tokens.shape
    rows_here, project_width = project.shape
    rest_width = 2 * N + step.shape[1]
    total = span * INNER
    flops = 2 * total * model * (project_width + rest_width)
    return pl.pallas_call(
        gather_kernel,
        out_shape=jax.ShapeDtypeStruct((total, project_width + rest_width), jnp.bfloat16),
        in_specs=[pl.BlockSpec(memory_space=pltpu.VMEM)] * 4,
        out_specs=pl.BlockSpec(memory_space=pltpu.VMEM),
        scratch_shapes=[
            pltpu.VMEM((INNER, span, model), jnp.bfloat16),
            pltpu.VMEM((rows_here * CTX, project_width), jnp.bfloat16),
            pltpu.VMEM((rows_here * CTX, rest_width), jnp.bfloat16),
            pltpu.VMEM((INNER, 2 * N // INNER, rows_here), jnp.bfloat16),
            pltpu.SemaphoreType.DMA,
            pltpu.SemaphoreType.DMA((QUARTERS * INNER,)),
            pltpu.SemaphoreType.DMA,
            pltpu.SemaphoreType.DMA((CTX,)),
            pltpu.SemaphoreType.DMA,
            pltpu.SemaphoreType.DMA((CTX,)),
            pltpu.SemaphoreType.DMA,
            pltpu.SemaphoreType.DMA,
        ],
        compiler_params=pltpu.CompilerParams(
            collective_id=0, has_side_effects=True, vmem_limit_bytes=VMEM_LIMIT
        ),
        cost_estimate=pl.CostEstimate(flops=flops, bytes_accessed=8 * 2**20, transcendentals=0),
        name="gather_project",
    )(tokens, project, state, step)


def lane_pair(values, first):
    width = 2 * P_SIZE
    low = lax.broadcasted_iota(jnp.int32, (values.shape[0], width), 1) < P_SIZE
    return jnp.where(low, values[:, first : first + 1], values[:, first + 1 : first + 2])


def per_channel(values, heads):
    return jnp.concatenate([lane_pair(values, h) for h in range(0, heads, 2)], axis=1)


def scan_kernel(
    heads,
    pre_ref,
    taps_ref,
    bias_ref,
    rate_ref,
    gain_ref,
    out_ref,
    tail,
    active,
    cums,
    steps,
    fresh,
    logs,
    diag,
    own_state,
    own_decay,
    in_state,
    in_decay,
    back,
    prior,
    gated,
    got,
    tail_send,
    tail_recv,
    decay_send,
    decay_recv,
    state_send,
    state_recv,
    back_send,
    back_recv,
    out_send,
    out_recv,
):
    ctx = lax.axis_index("ctx")
    inner = lax.axis_index("inner")
    width = heads * P_SIZE
    blocks = pre_ref.shape[0] // SPAN
    slices = CTX // 2
    piece = N * width // slices // (2 * P_SIZE)
    halves = width // (2 * P_SIZE)
    per_half = slices // halves
    z = ctx // 2
    scans = (ctx % 2) == (z % 2)

    def scanner(k):
        return 2 * k + k % 2

    barrier = pltpu.get_barrier_semaphore()

    def greet_inner(step, carry):
        pl.semaphore_signal(
            barrier, inc=1, device_id={"inner": (inner + step) % INNER}, device_id_type=MESH
        )
        return carry

    def greet_ctx(step, carry):
        pl.semaphore_signal(
            barrier, inc=1, device_id={"ctx": (ctx + step) % CTX}, device_id_type=MESH
        )
        return carry

    lax.fori_loop(1, INNER, greet_inner, 0)
    lax.fori_loop(1, CTX, greet_ctx, 0)
    pl.semaphore_wait(barrier, INNER - 1 + CTX - 1)

    conv_cols = slice(width, 2 * width + 2 * N)
    to_tail = remote(
        pre_ref.at[pl.ds((blocks - 1) * SPAN + SPAN - 16, 16), pl.ds(width, width + 2 * N)],
        tail,
        tail_send,
        tail_recv,
        {"ctx": (ctx + 1) % CTX},
    )
    to_tail.start()

    row = lax.broadcasted_iota(jnp.int32, (SPAN, SPAN), 0)
    col = lax.broadcasted_iota(jnp.int32, (SPAN, SPAN), 1)
    lower = col <= row
    ones = jnp.where(lower, 1.0, 0.0)

    def rows_of(c):
        return pl.ds(pl.multiple_of(c * SPAN, SPAN), SPAN)

    def decays(c, total):
        raw = pre_ref[rows_of(c), 2 * width + 2 * N :].astype(jnp.float32) + bias_ref[...]
        step = jnp.maximum(raw, 0.0) + jnp.log1p(jnp.exp(-jnp.abs(raw)))
        cum = jnp.dot(
            ones,
            step * rate_ref[...],
            precision=lax.Precision.HIGHEST,
            preferred_element_type=jnp.float32,
        )
        cums[c] = cum
        steps[c] = step
        logs[c] = jnp.broadcast_to(per_channel(total, heads), (8, width))
        return total + cum[SPAN - 1 :, :]

    total = lax.fori_loop(0, blocks, decays, jnp.zeros((1, SPAN), jnp.float32))
    decay_all = jnp.exp(per_channel(total, heads))
    for half in range(halves):
        own_decay[half] = jnp.broadcast_to(
            decay_all[:, half * 2 * P_SIZE : (half + 1) * 2 * P_SIZE], (8, 2 * P_SIZE)
        )

    def send_decay(k, carry):
        to = scanner(k)

        @pl.when(to != ctx)
        def _():
            remote(
                own_decay.at[k // per_half], in_decay.at[ctx], decay_send, decay_recv, {"ctx": to}
            ).start()

        return carry

    lax.fori_loop(0, slices, send_decay, 0)

    def convolve(c, previous):
        current = pre_ref[rows_of(c), conv_cols]
        extended = jnp.concatenate([previous, current], axis=0).astype(jnp.float32)
        mixed = jnp.broadcast_to(taps_ref[CONV : CONV + 1], current.shape)
        for k in range(CONV):
            begin = 16 - (CONV - 1) + k
            mixed = mixed + taps_ref[k : k + 1] * extended[begin : begin + SPAN]
        values = (mixed / (1.0 + jnp.exp(-mixed))).astype(jnp.bfloat16)
        active[rows_of(c)] = values
        cum, step = cums[c], steps[c]
        to_end = jnp.exp(cum[SPAN - 1 :] - cum) * step
        scaled = (values[:, :width].astype(jnp.float32) * per_channel(to_end, heads)).astype(
            jnp.bfloat16
        )
        fresh[c] = lax.dot_general(
            values[:, width : width + N],
            scaled,
            (((0,), (0,)), ((), ())),
            preferred_element_type=jnp.float32,
        )

    def convolve_later(c, carry):
        convolve(c, pre_ref[pl.ds(pl.multiple_of(c * SPAN - 16, 16), 16), conv_cols])
        return carry

    lax.fori_loop(1, blocks, convolve_later, 0)
    to_tail.wait_recv()
    edge = tail[...]
    convolve(0, jnp.where(ctx > 0, edge, jnp.zeros_like(edge)))

    def chain(c, state):
        added = fresh[c]
        fresh[c] = state
        return jnp.exp(per_channel(cums[c, SPAN - 1 :], heads)) * state + added

    state = lax.fori_loop(0, blocks, chain, jnp.zeros((N, width), jnp.float32))
    for half in range(halves):
        own_state[half] = state[:, half * 2 * P_SIZE : (half + 1) * 2 * P_SIZE].astype(jnp.bfloat16)

    def slice_of(k):
        return pl.ds(pl.multiple_of((k % per_half) * piece, piece), piece)

    def send_state(k, carry):
        to = scanner(k)

        @pl.when(to != ctx)
        def _():
            remote(
                own_state.at[k // per_half, slice_of(k)],
                in_state.at[ctx],
                state_send,
                state_recv,
                {"ctx": to},
            ).start()

        return carry

    lax.fori_loop(0, slices, send_state, 0)

    @pl.when(scans)
    def _():
        in_state[ctx] = own_state[z // per_half, slice_of(z)]
        in_decay[ctx] = own_decay[z // per_half]

    def inside(c, carry):
        values = active[rows_of(c)]
        cum, step = cums[c], steps[c]
        cum_rows, step_rows = cum.T, step.T
        scores = lax.dot_general(
            values[:, width + N :],
            values[:, width : width + N],
            (((1,), (1,)), ((), ())),
            preferred_element_type=jnp.float32,
        )
        lane = lax.broadcasted_iota(jnp.int32, (SPAN, 2 * P_SIZE), 1)
        for h in range(0, heads, 2):
            mixes, sides = [], []
            xs = values[:, h * P_SIZE : (h + 2) * P_SIZE]
            for side in range(2):
                at = h + side
                gap = jnp.where(lower, cum[:, at : at + 1] - cum_rows[at : at + 1], -jnp.inf)
                mix = scores * jnp.exp(gap) * step_rows[at : at + 1]
                mixes.append(mix.astype(jnp.bfloat16))
                sides.append(jnp.where((lane < P_SIZE) == (side == 0), xs, jnp.zeros_like(xs)))
            diag[c, :, h * P_SIZE : (h + 2) * P_SIZE] = jnp.dot(
                jnp.concatenate(mixes, axis=1),
                jnp.concatenate(sides, axis=0),
                preferred_element_type=jnp.float32,
            )
        return carry

    lax.fori_loop(0, blocks, inside, 0)

    @pl.when(scans)
    def _():
        landed(in_decay.at[pl.ds(0, CTX - 1)], decay_recv)
        landed(in_state.at[pl.ds(0, CTX - 1)], state_recv)

        def join(c, running):
            back[c] = running.astype(jnp.bfloat16)

            @pl.when(c != ctx)
            def _():
                remote(
                    back.at[c], prior.at[z // per_half, slice_of(z)], back_send, back_recv, {"ctx": c}
                ).start()

            return running * in_decay[c, :1] + in_state[c].astype(jnp.float32)

        lax.fori_loop(0, CTX, join, jnp.zeros((piece, 2 * P_SIZE), jnp.float32))
        prior[z // per_half, slice_of(z)] = back[ctx]
        landed(in_state.at[pl.ds(0, slices - 1)], back_recv)

    @pl.when(jnp.logical_not(scans))
    def _():
        landed(in_state.at[pl.ds(0, slices)], back_recv)

    before = jnp.concatenate([prior[half] for half in range(halves)], axis=1).astype(jnp.float32)

    def finish(turn, carry):
        c = (inner + 1 + turn) % INNER
        state_in = (fresh[c] + jnp.exp(logs[c, :1]) * before).astype(jnp.bfloat16)
        over = jnp.dot(
            active[rows_of(c), width + N :], state_in, preferred_element_type=jnp.float32
        )
        out = diag[c] + over * per_channel(jnp.exp(cums[c]), heads)
        gate = pre_ref[rows_of(c), :width].astype(jnp.float32)
        gated[c] = (out * (gate / (1.0 + jnp.exp(-gate)))).astype(jnp.bfloat16)

        @pl.when(c != inner)
        def _():
            remote(gated.at[c], got.at[inner], out_send, out_recv, {"inner": c}).start()

        return carry

    lax.fori_loop(0, INNER, finish, 0)
    got[inner] = gated[inner]
    landed(got.at[pl.ds(0, INNER - 1)], out_recv)

    share = INNER // G
    for group in range(G):
        squares = jnp.zeros((SPAN, width), jnp.float32)
        for i in range(share):
            part = got[group * share + i].astype(jnp.float32)
            squares = squares + part * part
        power = jnp.sum(squares, axis=1, keepdims=True) / (H * P_SIZE // G)
        scale = lax.rsqrt(power + EPSILON)
        for i in range(share):
            lanes = slice((group * share + i) * width, (group * share + i + 1) * width)
            part = got[group * share + i].astype(jnp.float32)
            out_ref[:, lanes] = (part * scale * gain_ref[:, lanes]).astype(jnp.bfloat16)

    to_tail.wait_send()
    landed(gated.at[pl.ds(0, INNER - 1)], out_send)

    @pl.when(scans)
    def _():
        landed(in_decay.at[pl.ds(0, slices - 1)], decay_send)
        landed(in_state.at[pl.ds(0, slices - 1)], state_send)
        landed(back.at[pl.ds(0, CTX - 1)], back_send)

    @pl.when(jnp.logical_not(scans))
    def _():
        landed(in_decay.at[pl.ds(0, slices)], decay_send)
        landed(in_state.at[pl.ds(0, slices)], state_send)


def scan_gate(pre, taps, bias, rate, gain, heads):
    total = pre.shape[0]
    blocks = total // SPAN
    width = heads * P_SIZE
    slices = CTX // 2
    halves = width // (2 * P_SIZE)
    piece = N * width // slices // (2 * P_SIZE)
    vmem = pltpu.VMEM
    dma = pltpu.SemaphoreType.DMA
    return pl.pallas_call(
        functools.partial(scan_kernel, heads),
        out_shape=jax.ShapeDtypeStruct((total // INNER, INNER * width), jnp.bfloat16),
        in_specs=[pl.BlockSpec(memory_space=vmem)] * 5,
        out_specs=pl.BlockSpec(memory_space=vmem),
        scratch_shapes=[
            vmem((16, width + 2 * N), jnp.bfloat16),
            vmem((total, width + 2 * N), jnp.bfloat16),
            vmem((blocks, SPAN, SPAN), jnp.float32),
            vmem((blocks, SPAN, SPAN), jnp.float32),
            vmem((blocks, N, width), jnp.float32),
            vmem((blocks, 8, width), jnp.float32),
            vmem((blocks, SPAN, width), jnp.float32),
            vmem((halves, N, 2 * P_SIZE), jnp.bfloat16),
            vmem((halves, 8, 2 * P_SIZE), jnp.float32),
            vmem((CTX, piece, 2 * P_SIZE), jnp.bfloat16),
            vmem((CTX, 8, 2 * P_SIZE), jnp.float32),
            vmem((CTX, piece, 2 * P_SIZE), jnp.bfloat16),
            vmem((halves, N, 2 * P_SIZE), jnp.bfloat16),
            vmem((INNER, SPAN, width), jnp.bfloat16),
            vmem((INNER, SPAN, width), jnp.bfloat16),
        ]
        + [dma] * 10,
        compiler_params=pltpu.CompilerParams(
            collective_id=1, has_side_effects=True, vmem_limit_bytes=VMEM_LIMIT
        ),
        name="scan_gate",
    )(pre, taps, bias, rate, gain)


def pick_group(values, group):
    shaped = values.reshape(values.shape[:-1] + (N, G))
    return lax.dynamic_index_in_dim(shaped, group, shaped.ndim - 1, keepdims=False)


def on_device(
    tokens,
    project_weight,
    state_weight,
    step_weight,
    mixer_taps,
    state_taps,
    step_bias,
    decay_log,
    norm_gain,
):
    heads = step_weight.shape[1]
    group = lax.axis_index("inner") * heads // (H // G)
    rows_here = project_weight.shape[0]
    wide = project_weight.reshape(rows_here, -1)
    state = state_weight.reshape(rows_here, 2, -1, G).transpose(3, 1, 2, 0)
    state = state.reshape(G, -1, rows_here)
    step = jnp.pad(step_weight, ((0, 0), (0, SPAN - heads)))
    pre = gather_project(tokens, wide, state, step)
    taps = jnp.concatenate(
        [mixer_taps, pick_group(state_taps, group).reshape(CONV + 1, 2 * N)], axis=1
    )
    bias = jnp.pad(step_bias, (0, SPAN - heads))[None]
    rate = jnp.pad(-jnp.exp(decay_log), (0, SPAN - heads))[None]
    return scan_gate(pre, taps, bias, rate, norm_gain[None], heads)


def solution(mesh):
    placed = (
        P(("ctx", "inner"), None),
        P("ctx", None, "inner"),
        P("ctx", None, "inner"),
        P("ctx", "inner"),
        P(None, "inner"),
        P(),
        P("inner"),
        P("inner"),
        P(),
    )
    return jax.shard_map(
        on_device, mesh=mesh, in_specs=placed, out_specs=P(("ctx", "inner"), None), check_vma=False
    )
```

```python
import functools

import jax
import jax.numpy as jnp
from jax import lax
from jax.experimental import pallas as pl
from jax.experimental.pallas import tpu as pltpu
from jax.sharding import PartitionSpec as P

H = 64
P_SIZE = 64
N = 128
G = 4
CONV = 4
SPAN = 128
EPSILON = 1e-05
MESH = pl.DeviceIdType.MESH
CTX = 32
INNER = 16
SIDE = 4
QUARTERS = 4
VMEM_LIMIT = 60 * 1024 * 1024


def remote(src, dst, send_sem, recv_sem, device):
    return pltpu.make_async_remote_copy(
        src_ref=src,
        dst_ref=dst,
        send_sem=send_sem,
        recv_sem=recv_sem,
        device_id=device,
        device_id_type=MESH,
    )


def landed(ref, sem):
    pltpu.make_async_copy(ref, ref, sem).wait()


def mixer_kernel(
    heads,
    tok_ref,
    project_ref,
    state_ref,
    step_ref,
    mixer_ref,
    maps_ref,
    bias_ref,
    decay_ref,
    got,
    tokens,
    w_project,
    w_rest,
    pieces,
    parts,
    pre,
    taps,
    lead,
    tail,
    active,
    cums,
    steps,
    logs,
    fresh,
    diag,
    scaled_c,
    opened,
    own_state,
    in_state,
    back,
    prior,
    gated,
    tok_send,
    tok_recv,
    wp_send,
    wp_recv,
    wr_send,
    wr_recv,
    part_send,
    part_recv,
    tail_send,
    tail_recv,
    state_send,
    state_recv,
    back_send,
    back_recv,
    out_send,
    out_recv,
):
    ctx = lax.axis_index("ctx")
    inner = lax.axis_index("inner")
    y, x = inner // SIDE, inner % SIDE
    rows_here = project_ref.shape[0]
    group = inner // (INNER // G)
    width = heads * P_SIZE
    other = ctx + 1 - 2 * (ctx % 2)
    up, down = (ctx + 2) % CTX, (ctx + CTX - 2) % CTX

    def at(dy, dx):
        return ((y + dy) % SIDE) * SIDE + (x + dx) % SIDE

    barrier = pltpu.get_barrier_semaphore()

    def greet(step, carry):
        pl.semaphore_signal(
            barrier, inc=1, device_id={"inner": (inner + step) % INNER}, device_id_type=MESH
        )
        return carry

    lax.fori_loop(1, INNER, greet, 0)
    for peer in (up, down, other):
        pl.semaphore_signal(barrier, inc=1, device_id={"ctx": peer}, device_id_type=MESH)
    pl.semaphore_wait(barrier, INNER - 1 + 3)

    def one_hot(index, target):
        return jnp.where(index == target, 1.0, 0.0).astype(jnp.bfloat16)

    own_cols = state_ref.shape[0] * state_ref.shape[1]
    piece = N // INNER
    row = lax.broadcasted_iota(jnp.int32, (own_cols, own_cols), 0)
    col = lax.broadcasted_iota(jnp.int32, (own_cols, own_cols), 1)
    held = (row // piece % 2) * (own_cols // 2) + (row % piece) * G + row // (2 * piece)
    sorted_cols = jnp.dot(
        one_hot(held, col),
        state_ref[...].reshape(own_cols, rows_here),
        preferred_element_type=jnp.float32,
    ).astype(jnp.bfloat16)
    pieces[...] = sorted_cols.reshape(G, 2 * piece, rows_here)

    def part_copy(step):
        to = (inner + step) % INNER
        return remote(
            pieces.at[to // (INNER // G)],
            parts.at[inner],
            part_send,
            part_recv,
            {"inner": to},
        )

    def send_part(step, carry):
        part_copy(step).start()
        return carry

    lax.fori_loop(1, INNER, send_part, 0)
    parts[inner] = pieces[group]

    def rows_of(place):
        return pl.ds(pl.multiple_of(place * rows_here, rows_here), rows_here)

    def wp_copy(place, to):
        return remote(
            w_project.at[rows_of(place)],
            w_project.at[rows_of(place)],
            wp_send,
            wp_recv.at[place],
            {"ctx": to},
        )

    def wr_copy(place, to):
        return remote(
            w_rest.at[rows_of(place)],
            w_rest.at[rows_of(place)],
            wr_send,
            wr_recv.at[place],
            {"ctx": to},
        )

    w_project[rows_of(ctx), :width] = project_ref[:, 0, :]
    w_project[rows_of(ctx), width:] = project_ref[:, 1, :]
    for peer in (up, down, other):
        wp_copy(ctx, peer).start()

    quarter = tok_ref.shape[0] // QUARTERS

    def tok_send_to(q, held, move):
        rows = pl.ds(q * quarter, quarter)
        (dy, dx), (ay, ax) = held, move
        slot = ((dy - ay) % SIDE) * SIDE + (dx - ax) % SIDE
        mine = (dy % SIDE) * SIDE + dx % SIDE
        source = tok_ref.at[rows] if mine == 0 else tokens.at[mine, rows]
        remote(
            source,
            tokens.at[slot, rows],
            tok_send,
            tok_recv.at[q * INNER + slot],
            {"inner": at(ay, ax)},
        ).start()

    def tok_wait(q, held):
        slot = (held[0] % SIDE) * SIDE + held[1] % SIDE
        landed(tokens.at[slot, pl.ds(q * quarter, quarter)], tok_recv.at[q * INNER + slot])

    def turn(q, along, across):
        return (across, along) if q < 2 else (along, across)

    def sense(q):
        return 1 if q % 2 == 0 else -1

    for first in (True, False):
        for q in range(QUARTERS):
            for d in (sense(q), -sense(q)):
                tok_send_to(q, (0, 0), turn(q, d, 0) if first else turn(q, 0, d))
    tokens[0] = tok_ref[...]

    landed(parts.at[pl.ds(0, INNER - 1)], part_recv)
    row = lax.broadcasted_iota(jnp.int32, (2 * N, 2 * N), 0)
    col = lax.broadcasted_iota(jnp.int32, (2 * N, 2 * N), 1)
    goes = (row // piece % 2) * N + (row // (2 * piece)) * piece + row % piece
    state_cols = lax.dot_general(
        parts[...].reshape(2 * N, rows_here),
        one_hot(goes, col),
        (((0,), (0,)), ((), ())),
        preferred_element_type=jnp.float32,
    ).astype(jnp.bfloat16)
    row = lax.broadcasted_iota(jnp.int32, (heads, SPAN), 0)
    col = lax.broadcasted_iota(jnp.int32, (heads, SPAN), 1)
    step_cols = lax.dot_general(
        step_ref[...],
        one_hot(row, col),
        (((0,), (0,)), ((), ())),
        preferred_element_type=jnp.float32,
    ).astype(jnp.bfloat16)
    w_rest[rows_of(ctx), : 2 * N] = state_cols
    w_rest[rows_of(ctx), 2 * N :] = step_cols
    for peer in (up, down, other):
        wr_copy(ctx, peer).start()

    row = lax.broadcasted_iota(jnp.int32, (G * N, N), 0)
    col = lax.broadcasted_iota(jnp.int32, (G * N, N), 1)
    pick = jnp.where(row == col * G + group, 1.0, 0.0)
    taps[: CONV + 1, :width] = mixer_ref[...]
    for side in range(2):
        taps[: CONV + 1, width + side * N : width + (side + 1) * N] = jnp.dot(
            maps_ref[:, side, :],
            pick,
            precision=lax.Precision.HIGHEST,
            preferred_element_type=jnp.float32,
        )
    lanes = jnp.zeros((1, SPAN - heads), jnp.float32)
    bias = jnp.concatenate([bias_ref[...], lanes], axis=1)
    rate = jnp.concatenate([-jnp.exp(decay_ref[...]), lanes], axis=1)

    def relay(copy, recv, ref, hop):
        behind, ahead = (ctx + CTX - 2 * hop) % CTX, (ctx + 2 * hop) % CTX
        landed(ref.at[rows_of(behind)], recv.at[behind])
        if hop < CTX // 4:
            copy(behind, up).start()
        copy(behind, other).start()
        if hop < CTX // 4:
            landed(ref.at[rows_of(ahead)], recv.at[ahead])
            if hop < CTX // 4 - 1:
                copy(ahead, down).start()
            copy(ahead, other).start()

    def w_relay(hop):
        relay(wp_copy, wp_recv, w_project, hop)
        relay(wr_copy, wr_recv, w_rest, hop)

    def arrive(q, along, across):
        d = sense(q)
        held = turn(q, along, across)
        tok_wait(q, held)
        if across == 0:
            if along == -d:
                tok_send_to(q, held, turn(q, d, 0))
            for e in (d, -d):
                tok_send_to(q, held, turn(q, 0, e))
        elif across == -d:
            tok_send_to(q, held, turn(q, 0, d))

    for q in range(QUARTERS):
        arrive(q, -sense(q), 0)
        arrive(q, sense(q), 0)
        if q % 2:
            w_relay(1 + q // 2)
    for q in range(QUARTERS):
        arrive(q, 2, 0)
        arrive(q, 0, -sense(q))
        if q % 2:
            w_relay(3 + q // 2)
    for step in (-1, 1):
        for q in range(QUARTERS):
            arrive(q, step * sense(q), -sense(q))
        w_relay(5 + (step + 1) // 2)
    for q in range(QUARTERS):
        arrive(q, 2, -sense(q))
    w_relay(7)
    w_relay(8)

    def handed(hop, carry):
        src = (other + 2 * hop) % CTX
        landed(w_project.at[rows_of(src)], wp_recv.at[src])
        landed(w_rest.at[rows_of(src)], wr_recv.at[src])
        return carry

    lax.fori_loop(0, CTX // 2, handed, 0)

    project_width = w_project.shape[1]
    span = tok_ref.shape[0]
    blocks = pre.shape[0] // SPAN
    conv_cols = slice(width, 2 * width + 2 * N)
    row = lax.broadcasted_iota(jnp.int32, (SPAN, SPAN), 0)
    col = lax.broadcasted_iota(jnp.int32, (SPAN, SPAN), 1)
    lower = col <= row
    ones = jnp.where(lower, 1.0, 0.0)
    to_tail = remote(
        pre.at[pl.ds(blocks * SPAN - 16, 16), pl.ds(width, width + 2 * N)],
        tail,
        tail_send,
        tail_recv,
        {"ctx": (ctx + 1) % CTX},
    )

    def span_of(c):
        return pl.ds(pl.multiple_of(c * SPAN, SPAN), SPAN)

    def head_of(h):
        return slice(h * P_SIZE, (h + 1) * P_SIZE)

    def pair_of(h):
        return slice(h * P_SIZE, (h + 2) * P_SIZE)

    def silu(v):
        return v / (1.0 + jnp.exp(-v))

    def local(c):
        @pl.when(c == 0)
        def _():
            to_tail.wait_recv()
            edge = tail[...]
            lead[...] = jnp.where(ctx > 0, edge, jnp.zeros_like(edge))

        @pl.when(c > 0)
        def _():
            begin = pl.multiple_of(jnp.maximum(c * SPAN - 16, 0), 16)
            lead[...] = pre[pl.ds(begin, 16), conv_cols]

        raw = pre[span_of(c), 2 * width + 2 * N :].astype(jnp.float32) + bias
        step = jnp.maximum(raw, 0.0) + jnp.log1p(jnp.exp(-jnp.abs(raw)))
        cum = jnp.dot(
            ones,
            step * rate,
            precision=lax.Precision.HIGHEST,
            preferred_element_type=jnp.float32,
        )
        cums[c] = cum
        steps[c] = step
        current = pre[span_of(c), conv_cols]
        extended = jnp.concatenate([lead[...], current], axis=0).astype(jnp.float32)
        mixed = jnp.broadcast_to(taps[CONV : CONV + 1], current.shape)
        for k in range(CONV):
            begin = 16 - (CONV - 1) + k
            mixed = mixed + taps[k : k + 1] * extended[begin : begin + SPAN]
        values = silu(mixed).astype(jnp.bfloat16)
        active[span_of(c)] = values
        to_end = jnp.exp(cum[SPAN - 1 :] - cum) * step
        xs = values[:, :width].astype(jnp.float32).T.astype(jnp.bfloat16)
        bs = values[:, width : width + N].astype(jnp.float32)
        for h in range(heads):
            weighted = (bs * to_end[:, h : h + 1]).astype(jnp.bfloat16)
            fresh[c, head_of(h)] = jnp.dot(
                xs[head_of(h)], weighted, preferred_element_type=jnp.float32
            )

    def inside(c):
        values = active[span_of(c)]
        cum, step = cums[c], steps[c]
        cum_rows, step_rows = cum.T, step.T
        scores = lax.dot_general(
            values[:, width + N :],
            values[:, width : width + N],
            (((1,), (1,)), ((), ())),
            preferred_element_type=jnp.float32,
        )
        cs = values[:, width + N :].astype(jnp.float32)
        begun = jnp.exp(cum)
        lane = lax.broadcasted_iota(jnp.int32, (SPAN, 2 * P_SIZE), 1)
        for h in range(0, heads, 2):
            mixes, sides = [], []
            xs = values[:, pair_of(h)]
            for side in range(2):
                at_h = h + side
                gap = jnp.where(lower, cum[:, at_h : at_h + 1] - cum_rows[at_h : at_h + 1], -jnp.inf)
                mix = scores * jnp.exp(gap) * step_rows[at_h : at_h + 1]
                mixes.append(mix.astype(jnp.bfloat16))
                sides.append(jnp.where((lane < P_SIZE) == (side == 0), xs, jnp.zeros_like(xs)))
                scaled_c[span_of(c), at_h * N : (at_h + 1) * N] = (
                    cs * begun[:, at_h : at_h + 1]
                ).astype(jnp.bfloat16)
            diag[c, :, pair_of(h)] = jnp.dot(
                jnp.concatenate(mixes, axis=1),
                jnp.concatenate(sides, axis=0),
                preferred_element_type=jnp.float32,
            )
        opened[c] = silu(pre[span_of(c), :width].astype(jnp.float32))

    done = set()
    for q in range(QUARTERS):
        for along, across in ((-1, 0), (1, 0), (2, 0)):
            done.add((q,) + tuple(v % SIDE for v in turn(q, along, across)))
        for along in range(SIDE):
            done.add((q,) + tuple(v % SIDE for v in turn(q, along, -sense(q))))
    for dy, firsts in ((0, ()), (1, (1,)), (3, (0,)), (2, (2, 3))):
        for dx in range(SIDE):
            for q in range(QUARTERS):
                if (dy, dx) != (0, 0) and (q, dy, dx) not in done:
                    tok_wait(q, (dy, dx))

        def multiply(pair, carry, dy=dy):
            first = dy * SIDE + 2 * pair
            rows = tokens[pl.ds(first, 2)].reshape(2 * span, tokens.shape[2])
            wide = jnp.dot(rows, w_project[...], preferred_element_type=jnp.float32).astype(
                jnp.bfloat16
            )
            rest = jnp.dot(rows, w_rest[...], preferred_element_type=jnp.float32).astype(
                jnp.bfloat16
            )
            for half in range(2):
                to = span_of(at(dy, 2 * pair + half))
                pre[to, :project_width] = wide[half * span : (half + 1) * span]
                pre[to, project_width:] = rest[half * span : (half + 1) * span]
            return carry

        lax.fori_loop(0, SIDE // 2, multiply, 0)
        here = (y + dy) % SIDE

        @pl.when(here == SIDE - 1)
        def _():
            to_tail.start()

        def block_at(i, here=here, firsts=firsts):
            c = here * SIDE + 1 + i
            for n, f in enumerate(firsts):
                c = jnp.where(i == SIDE - 1 + n, ((y + f) % SIDE) * SIDE, c)
            return c

        last = len(firsts) == 2

        def work(i, carry, block_at=block_at, last=last):
            local(block_at(i))
            if not last:
                inside(block_at(i))
            return carry

        lax.fori_loop(0, SIDE - 1 + len(firsts), work, 0)

    def chain(c, carry):
        state, total = carry
        end = cums[c, SPAN - 1 :]
        logs[c] = jnp.broadcast_to(total, (8, SPAN))
        keep = jnp.exp(end)
        later = []
        for h in range(heads):
            later.append(keep[:, h : h + 1] * state[head_of(h)] + fresh[c, head_of(h)])
        fresh[c] = state
        return jnp.concatenate(later, axis=0), total + end

    state, total = lax.fori_loop(
        0, blocks, chain, (jnp.zeros((width, N), jnp.float32), jnp.zeros((1, SPAN), jnp.float32))
    )
    slices = CTX // 2
    deep = width // slices
    z = ctx // 2
    scans = (ctx % 2) == (z % 2)

    def scanner(k):
        return 2 * k + k % 2

    decay = jnp.exp(total)
    third = lax.broadcasted_iota(jnp.int32, (deep, N), 0)
    for h in range(heads):
        whole = jnp.broadcast_to(decay[:, h : h + 1], (deep, N))
        high = whole.astype(jnp.bfloat16).astype(jnp.float32)
        middle = (whole - high).astype(jnp.bfloat16).astype(jnp.float32)
        low = whole - high - middle
        packed = jnp.where(
            third == 0, high, jnp.where(third == 1, middle, jnp.where(third == 2, low, 0.0))
        ).astype(jnp.bfloat16)
        for k in range(h * P_SIZE // deep, (h + 1) * P_SIZE // deep):
            own_state[k, :deep] = state[k * deep : (k + 1) * deep].astype(jnp.bfloat16)
            own_state[k, deep:] = packed

    def send_state(turned, carry):
        k = (z + turned) % slices
        to = scanner(k)

        @pl.when(to != ctx)
        def _():
            remote(
                own_state.at[k], in_state.at[ctx], state_send, state_recv, {"ctx": to}
            ).start()

        return carry

    lax.fori_loop(0, slices, send_state, 0)

    @pl.when(scans)
    def _():
        in_state[ctx] = own_state[z]

    def rest_inside(i, carry):
        inside(block_at(i))
        return carry

    lax.fori_loop(0, SIDE + 1, rest_inside, 0)

    @pl.when(scans)
    def _():
        landed(in_state.at[pl.ds(0, CTX - 1)], state_recv)

        def join(c, running):
            back[c] = running.astype(jnp.bfloat16)

            @pl.when(c != ctx)
            def _():
                remote(back.at[c], prior.at[z], back_send, back_recv, {"ctx": c}).start()

            came = in_state[c].astype(jnp.float32)
            keep = came[deep : deep + 1] + came[deep + 1 : deep + 2] + came[deep + 2 : deep + 3]
            return running * keep + came[:deep]

        lax.fori_loop(0, CTX, join, jnp.zeros((deep, N), jnp.float32))
        prior[z] = back[ctx]
        landed(prior.at[pl.ds(0, slices - 1)], back_recv)

    @pl.when(jnp.logical_not(scans))
    def _():
        landed(prior, back_recv)

    before = prior[...].astype(jnp.float32).reshape(width, N)
    low_rows = lax.broadcasted_iota(jnp.int32, (2 * P_SIZE, N), 0) < P_SIZE

    def finish(turned, carry):
        c = (inner + 1 + turned) % INNER
        reach = jnp.exp(logs[c, :1])
        for h in range(0, heads, 2):
            carried = jnp.where(low_rows, reach[:, h : h + 1], reach[:, h + 1 : h + 2])
            entered = fresh[c, pair_of(h)] + carried * before[pair_of(h)]
            high = entered.astype(jnp.bfloat16)
            low = (entered - high.astype(jnp.float32)).astype(jnp.bfloat16)
            over = diag[c, :, pair_of(h)]
            for share in (high, low):
                none = jnp.zeros_like(share)
                over = over + lax.dot_general(
                    scaled_c[span_of(c), h * N : (h + 2) * N],
                    jnp.concatenate(
                        [jnp.where(low_rows, share, none), jnp.where(low_rows, none, share)], axis=1
                    ),
                    (((1,), (1,)), ((), ())),
                    preferred_element_type=jnp.float32,
                )
            gated[c, :, pair_of(h)] = (over * opened[c, :, pair_of(h)]).astype(jnp.bfloat16)

        @pl.when(c != inner)
        def _():
            remote(gated.at[c], got.at[inner], out_send, out_recv, {"inner": c}).start()

        return carry

    lax.fori_loop(0, INNER, finish, 0)
    got[inner] = gated[inner]

    landed(tokens.at[pl.ds(0, INNER - 1)], tok_send)
    landed(parts.at[pl.ds(0, INNER - 1)], part_send)
    sent = rows_here * (2 + 1 + 7 + 6 + 15)
    landed(w_project.at[pl.ds(0, sent)], wp_send)
    landed(w_rest.at[pl.ds(0, sent)], wr_send)
    to_tail.wait_send()

    @pl.when(scans)
    def _():
        landed(own_state.at[pl.ds(0, slices - 1)], state_send)
        landed(back.at[pl.ds(0, CTX - 1)], back_send)

    @pl.when(jnp.logical_not(scans))
    def _():
        landed(own_state, state_send)

    landed(gated.at[pl.ds(0, INNER - 1)], out_send)
    landed(got.at[pl.ds(0, INNER - 1)], out_recv)


def norm_kernel(got, gain_ref, out_ref):
    span, width = got.shape[1], got.shape[2]
    share = INNER // G
    for group in range(G):
        squares = jnp.zeros((span, width), jnp.float32)
        for i in range(share):
            part = got[group * share + i].astype(jnp.float32)
            squares = squares + part * part
        power = jnp.sum(squares, axis=1, keepdims=True) / (share * width)
        scale = lax.rsqrt(power + EPSILON)
        for i in range(share):
            lanes = slice((group * share + i) * width, (group * share + i + 1) * width)
            part = got[group * share + i].astype(jnp.float32)
            out_ref[:, lanes] = (part * scale * gain_ref[:, lanes]).astype(jnp.bfloat16)


def on_device(
    tokens,
    project_weight,
    state_weight,
    step_weight,
    mixer_taps,
    state_taps,
    step_bias,
    decay_log,
    norm_gain,
):
    heads = step_weight.shape[1]
    rows_here = project_weight.shape[0]
    span, model = tokens.shape
    width = heads * P_SIZE
    total = span * INNER
    blocks = total // SPAN
    slices = CTX // 2
    deep = width // slices
    rest = 2 * N + SPAN
    vmem = pltpu.VMEM
    dma = pltpu.SemaphoreType.DMA
    bf16, f32 = jnp.bfloat16, jnp.float32
    got = pl.pallas_call(
        functools.partial(mixer_kernel, heads),
        out_shape=jax.ShapeDtypeStruct((INNER, span, width), bf16),
        in_specs=[pl.BlockSpec(memory_space=vmem)] * 8,
        out_specs=pl.BlockSpec(memory_space=vmem),
        scratch_shapes=[
            vmem((INNER, span, model), bf16),
            vmem((rows_here * CTX, 2 * width), bf16),
            vmem((rows_here * CTX, rest), bf16),
            vmem((G, 2 * N // INNER, rows_here), bf16),
            vmem((INNER, 2 * N // INNER, rows_here), bf16),
            vmem((total, 2 * width + rest), bf16),
            vmem((8, width + 2 * N), f32),
            vmem((16, width + 2 * N), bf16),
            vmem((16, width + 2 * N), bf16),
            vmem((total, width + 2 * N), bf16),
            vmem((blocks, SPAN, SPAN), f32),
            vmem((blocks, SPAN, SPAN), f32),
            vmem((blocks, 8, SPAN), f32),
            vmem((blocks, width, N), f32),
            vmem((blocks, SPAN, width), f32),
            vmem((total, heads * N), bf16),
            vmem((blocks, SPAN, width), f32),
            vmem((slices, 2 * deep, N), bf16),
            vmem((CTX, 2 * deep, N), bf16),
            vmem((CTX, deep, N), bf16),
            vmem((slices, deep, N), bf16),
            vmem((INNER, SPAN, width), bf16),
            dma,
            dma((QUARTERS * INNER,)),
            dma,
            dma((CTX,)),
            dma,
            dma((CTX,)),
        ]
        + [dma] * 10,
        compiler_params=pltpu.CompilerParams(
            collective_id=0, has_side_effects=True, vmem_limit_bytes=VMEM_LIMIT
        ),
        name="mixer",
    )(
        tokens,
        project_weight,
        state_weight.transpose(1, 2, 0),
        step_weight.T,
        mixer_taps,
        state_taps,
        step_bias[None],
        decay_log[None],
    )
    return pl.pallas_call(
        norm_kernel,
        out_shape=jax.ShapeDtypeStruct((span, INNER * width), bf16),
        in_specs=[pl.BlockSpec(memory_space=vmem)] * 2,
        out_specs=pl.BlockSpec(memory_space=vmem),
        name="norm",
    )(got, norm_gain[None])


def solution(mesh):
    placed = (
        P(("ctx", "inner"), None),
        P("ctx", None, "inner"),
        P("ctx", None, "inner"),
        P("ctx", "inner"),
        P(None, "inner"),
        P(),
        P("inner"),
        P("inner"),
        P(),
    )
    return jax.shard_map(
        on_device, mesh=mesh, in_specs=placed, out_specs=P(("ctx", "inner"), None), check_vma=False
    )
```

```python
import functools

import jax
import jax.numpy as jnp
from jax import lax
from jax.experimental import pallas as pl
from jax.experimental.pallas import tpu as pltpu
from jax.sharding import PartitionSpec as P

H = 64
P_SIZE = 64
N = 128
G = 4
CONV = 4
SPAN = 128
EPSILON = 1e-05
MESH = pl.DeviceIdType.MESH
CTX = 32
INNER = 16
SIDE = 4
QUARTERS = 4
VMEM_LIMIT = 60 * 1024 * 1024


def remote(src, dst, send_sem, recv_sem, device):
    return pltpu.make_async_remote_copy(
        src_ref=src,
        dst_ref=dst,
        send_sem=send_sem,
        recv_sem=recv_sem,
        device_id=device,
        device_id_type=MESH,
    )


def landed(ref, sem):
    pltpu.make_async_copy(ref, ref, sem).wait()


def mixer_kernel(
    heads,
    tok_ref,
    project_ref,
    state_ref,
    step_ref,
    mixer_ref,
    maps_ref,
    bias_ref,
    decay_ref,
    got,
    tokens,
    w_project,
    w_rest,
    pieces,
    parts,
    pre,
    taps,
    lead,
    tail,
    active,
    cums,
    steps,
    logs,
    fresh,
    diag,
    scaled_c,
    opened,
    own_state,
    in_state,
    back,
    prior,
    gated,
    tok_send,
    tok_recv,
    wp_swap,
    wr_swap,
    wp_send,
    wp_recv,
    wr_send,
    wr_recv,
    part_send,
    part_recv,
    tail_send,
    tail_recv,
    state_send,
    state_recv,
    back_send,
    back_recv,
    out_send,
    out_recv,
):
    ctx = lax.axis_index("ctx")
    inner = lax.axis_index("inner")
    y, x = inner // SIDE, inner % SIDE
    rows_here = project_ref.shape[0]
    group = inner // (INNER // G)
    width = heads * P_SIZE
    other = ctx + 1 - 2 * (ctx % 2)
    up, down = (ctx + 2) % CTX, (ctx + CTX - 2) % CTX

    def at(dy, dx):
        return ((y + dy) % SIDE) * SIDE + (x + dx) % SIDE

    core = ctx % 2
    z = ctx // 2
    depth = CTX // 2
    way = 1 - 2 * core
    onward = (ctx + CTX + 2 * way) % CTX

    barrier = pltpu.get_barrier_semaphore()

    def greet(step, carry):
        pl.semaphore_signal(
            barrier, inc=1, device_id={"inner": (inner + step) % INNER}, device_id_type=MESH
        )
        return carry

    lax.fori_loop(1, INNER, greet, 0)
    for peer in (up, down, other):
        pl.semaphore_signal(barrier, inc=1, device_id={"ctx": peer}, device_id_type=MESH)

    def one_hot(index, target):
        return jnp.where(index == target, 1.0, 0.0).astype(jnp.bfloat16)

    def rows_of(place):
        return pl.ds(pl.multiple_of(place * rows_here, rows_here), rows_here)

    w_project[rows_of(ctx), :width] = project_ref[:, 0, :]
    w_project[rows_of(ctx), width:] = project_ref[:, 1, :]
    own_cols = state_ref.shape[0] * state_ref.shape[1]
    piece = N // INNER
    row = lax.broadcasted_iota(jnp.int32, (own_cols, own_cols), 0)
    col = lax.broadcasted_iota(jnp.int32, (own_cols, own_cols), 1)
    held = (row // piece % 2) * (own_cols // 2) + (row % piece) * G + row // (2 * piece)
    sorted_cols = jnp.dot(
        one_hot(held, col),
        state_ref[...].reshape(own_cols, rows_here),
        preferred_element_type=jnp.float32,
    ).astype(jnp.bfloat16)
    pieces[...] = sorted_cols.reshape(G, 2 * piece, rows_here)
    parts[inner] = pieces[group]
    row = lax.broadcasted_iota(jnp.int32, (heads, SPAN), 0)
    col = lax.broadcasted_iota(jnp.int32, (heads, SPAN), 1)
    w_rest[rows_of(ctx), 2 * N :] = lax.dot_general(
        step_ref[...],
        one_hot(row, col),
        (((0,), (0,)), ((), ())),
        preferred_element_type=jnp.float32,
    ).astype(jnp.bfloat16)
    row = lax.broadcasted_iota(jnp.int32, (G * N, N), 0)
    col = lax.broadcasted_iota(jnp.int32, (G * N, N), 1)
    pick = jnp.where(row == col * G + group, 1.0, 0.0)
    taps[: CONV + 1, :width] = mixer_ref[...]
    for side in range(2):
        taps[: CONV + 1, width + side * N : width + (side + 1) * N] = jnp.dot(
            maps_ref[:, side, :],
            pick,
            precision=lax.Precision.HIGHEST,
            preferred_element_type=jnp.float32,
        )
    lanes = jnp.zeros((1, SPAN - heads), jnp.float32)
    bias = jnp.concatenate([bias_ref[...], lanes], axis=1)
    rate = jnp.concatenate([-jnp.exp(decay_ref[...]), lanes], axis=1)
    tokens[0] = tok_ref[...]
    row = lax.broadcasted_iota(jnp.int32, (2 * N, 2 * N), 0)
    col = lax.broadcasted_iota(jnp.int32, (2 * N, 2 * N), 1)
    goes = one_hot((row // piece % 2) * N + (row // (2 * piece)) * piece + row % piece, col)

    pl.semaphore_wait(barrier, INNER - 1 + 3)

    def swap(ref, sems):
        return remote(
            ref.at[rows_of(ctx)], ref.at[rows_of(ctx)], sems.at[0], sems.at[1], {"ctx": other}
        )

    def swapped(ref, sems):
        landed(ref.at[rows_of(other)], sems.at[1])

    def w_copy(ref, place, to, send, recv):
        return remote(ref.at[rows_of(place)], ref.at[rows_of(place)], send, recv.at[place], {"ctx": to})

    def wp_copy(place, to):
        return w_copy(w_project, place, to, wp_send, wp_recv)

    def wr_copy(place, to):
        return w_copy(w_rest, place, to, wr_send, wr_recv)

    wp_copy(ctx, onward).start()
    swap(w_project, wp_swap).start()

    def send_part(step, carry):
        to = (inner + step) % INNER
        remote(
            pieces.at[to // (INNER // G)], parts.at[inner], part_send, part_recv, {"inner": to}
        ).start()
        return carry

    lax.fori_loop(1, INNER, send_part, 0)

    quarter = tok_ref.shape[0] // QUARTERS

    def tok_send_to(q, held, move):
        rows = pl.ds(q * quarter, quarter)
        (dy, dx), (ay, ax) = held, move
        slot = ((dy - ay) % SIDE) * SIDE + (dx - ax) % SIDE
        mine = (dy % SIDE) * SIDE + dx % SIDE
        source = tok_ref.at[rows] if mine == 0 else tokens.at[mine, rows]
        remote(
            source,
            tokens.at[slot, rows],
            tok_send,
            tok_recv.at[q * INNER + slot],
            {"inner": at(ay, ax)},
        ).start()

    def tok_wait(q, held):
        slot = (held[0] % SIDE) * SIDE + held[1] % SIDE
        landed(tokens.at[slot, pl.ds(q * quarter, quarter)], tok_recv.at[q * INNER + slot])

    def turn(q, along, across):
        return (across, along) if q < 2 else (along, across)

    def sense(q):
        return 1 if q % 2 == 0 else -1

    for q in range(QUARTERS):
        for d in (sense(q), -sense(q)):
            tok_send_to(q, (0, 0), turn(q, d, 0))
    swapped(w_project, wp_swap)
    wp_copy(other, onward).start()
    for q in range(QUARTERS):
        for d in (sense(q), -sense(q)):
            tok_send_to(q, (0, 0), turn(q, 0, d))

    landed(parts.at[pl.ds(0, INNER - 1)], part_recv)
    w_rest[rows_of(ctx), : 2 * N] = lax.dot_general(
        parts[...].reshape(2 * N, rows_here),
        goes,
        (((0,), (0,)), ((), ())),
        preferred_element_type=jnp.float32,
    ).astype(jnp.bfloat16)
    wr_copy(ctx, onward).start()
    swap(w_rest, wr_swap).start()

    def relay(copy, recv, ref, hop):
        def step():
            chip = (z + depth - way * hop) % depth
            for place in (2 * chip + core, 2 * chip + 1 - core):
                landed(ref.at[rows_of(place)], recv.at[place])
                if hop < depth // 2 - 1:
                    copy(place, onward).start()
                elif hop == depth // 2 - 1:

                    @pl.when(core == 0)
                    def _():
                        copy(place, onward).start()

                copy(place, other).start()

        if hop < depth // 2:
            step()
        else:
            pl.when(core == 0)(step)

    def wp_relay(hop):
        relay(wp_copy, wp_recv, w_project, hop)

    def wr_relay(hop):
        relay(wr_copy, wr_recv, w_rest, hop)

    def w_relay(hop):
        wp_relay(hop)
        wr_relay(hop)

    def arrive(q, along, across):
        d = sense(q)
        held = turn(q, along, across)
        tok_wait(q, held)
        if across == 0:
            if along == -d:
                tok_send_to(q, held, turn(q, d, 0))
            for e in (d, -d):
                tok_send_to(q, held, turn(q, 0, e))
        elif across == -d:
            tok_send_to(q, held, turn(q, 0, d))

    for q in range(QUARTERS):
        arrive(q, -sense(q), 0)
    wp_relay(1)
    swapped(w_rest, wr_swap)
    wr_copy(other, onward).start()
    for q in range(QUARTERS):
        arrive(q, sense(q), 0)
    wr_relay(1)
    w_relay(2)
    for q in range(QUARTERS):
        arrive(q, 0, -sense(q))
    w_relay(3)
    for q in range(QUARTERS):
        arrive(q, 2, 0)
    w_relay(4)
    w_relay(5)
    for q in range(QUARTERS):
        arrive(q, -sense(q), -sense(q))
    w_relay(6)
    w_relay(7)
    for q in range(QUARTERS):
        arrive(q, sense(q), -sense(q))
    w_relay(8)
    for q in range(QUARTERS):
        arrive(q, 2, -sense(q))

    def handed(hop, carry):
        chip = (z + depth + way * hop) % depth
        for place in (2 * chip, 2 * chip + 1):
            landed(w_project.at[rows_of(place)], wp_recv.at[place])
            landed(w_rest.at[rows_of(place)], wr_recv.at[place])
        return carry

    lax.fori_loop(1, depth // 2, handed, 0)

    @pl.when(core == 1)
    def _():
        handed(depth // 2, 0)

    project_width = w_project.shape[1]
    span = tok_ref.shape[0]
    blocks = pre.shape[0] // SPAN
    conv_cols = slice(width, 2 * width + 2 * N)
    row = lax.broadcasted_iota(jnp.int32, (SPAN, SPAN), 0)
    col = lax.broadcasted_iota(jnp.int32, (SPAN, SPAN), 1)
    lower = col <= row
    ones = jnp.where(lower, 1.0, 0.0)
    to_tail = remote(
        pre.at[pl.ds(blocks * SPAN - 16, 16), pl.ds(width, width + 2 * N)],
        tail,
        tail_send,
        tail_recv,
        {"ctx": (ctx + 1) % CTX},
    )

    def span_of(c):
        return pl.ds(pl.multiple_of(c * SPAN, SPAN), SPAN)

    def head_of(h):
        return slice(h * P_SIZE, (h + 1) * P_SIZE)

    def pair_of(h):
        return slice(h * P_SIZE, (h + 2) * P_SIZE)

    def silu(v):
        return v / (1.0 + jnp.exp(-v))

    def local(c):
        @pl.when(c == 0)
        def _():
            to_tail.wait_recv()
            edge = tail[...]
            lead[...] = jnp.where(ctx > 0, edge, jnp.zeros_like(edge))

        @pl.when(c > 0)
        def _():
            begin = pl.multiple_of(jnp.maximum(c * SPAN - 16, 0), 16)
            lead[...] = pre[pl.ds(begin, 16), conv_cols]

        raw = pre[span_of(c), 2 * width + 2 * N :].astype(jnp.float32) + bias
        step = jnp.maximum(raw, 0.0) + jnp.log1p(jnp.exp(-jnp.abs(raw)))
        cum = jnp.dot(
            ones,
            step * rate,
            precision=lax.Precision.HIGHEST,
            preferred_element_type=jnp.float32,
        )
        cums[c] = cum
        steps[c] = step
        current = pre[span_of(c), conv_cols]
        extended = jnp.concatenate([lead[...], current], axis=0).astype(jnp.float32)
        mixed = jnp.broadcast_to(taps[CONV : CONV + 1], current.shape)
        for k in range(CONV):
            begin = 16 - (CONV - 1) + k
            mixed = mixed + taps[k : k + 1] * extended[begin : begin + SPAN]
        values = silu(mixed).astype(jnp.bfloat16)
        active[span_of(c)] = values
        to_end = jnp.exp(cum[SPAN - 1 :] - cum) * step
        xs = values[:, :width].astype(jnp.float32).T.astype(jnp.bfloat16)
        bs = values[:, width : width + N].astype(jnp.float32)
        for h in range(heads):
            weighted = (bs * to_end[:, h : h + 1]).astype(jnp.bfloat16)
            fresh[c, head_of(h)] = jnp.dot(
                xs[head_of(h)], weighted, preferred_element_type=jnp.float32
            )

    def inside(c):
        values = active[span_of(c)]
        cum, step = cums[c], steps[c]
        cum_rows, step_rows = cum.T, step.T
        scores = lax.dot_general(
            values[:, width + N :],
            values[:, width : width + N],
            (((1,), (1,)), ((), ())),
            preferred_element_type=jnp.float32,
        )
        cs = values[:, width + N :].astype(jnp.float32)
        begun = jnp.exp(cum)
        lane = lax.broadcasted_iota(jnp.int32, (SPAN, 2 * P_SIZE), 1)
        for h in range(0, heads, 2):
            mixes, sides = [], []
            xs = values[:, pair_of(h)]
            for side in range(2):
                at_h = h + side
                gap = jnp.where(lower, cum[:, at_h : at_h + 1] - cum_rows[at_h : at_h + 1], -jnp.inf)
                mix = scores * jnp.exp(gap) * step_rows[at_h : at_h + 1]
                mixes.append(mix.astype(jnp.bfloat16))
                sides.append(jnp.where((lane < P_SIZE) == (side == 0), xs, jnp.zeros_like(xs)))
                scaled_c[span_of(c), at_h * N : (at_h + 1) * N] = (
                    cs * begun[:, at_h : at_h + 1]
                ).astype(jnp.bfloat16)
            diag[c, :, pair_of(h)] = jnp.dot(
                jnp.concatenate(mixes, axis=1),
                jnp.concatenate(sides, axis=0),
                preferred_element_type=jnp.float32,
            )
        opened[c] = silu(pre[span_of(c), :width].astype(jnp.float32))

    done = set()
    for q in range(QUARTERS):
        for along, across in ((-1, 0), (1, 0), (2, 0)):
            done.add((q,) + tuple(v % SIDE for v in turn(q, along, across)))
        for along in range(SIDE):
            done.add((q,) + tuple(v % SIDE for v in turn(q, along, -sense(q))))
    for dy, firsts in ((0, ()), (1, (1,)), (3, (0,)), (2, (2, 3))):
        for dx in range(SIDE):
            for q in range(QUARTERS):
                if (dy, dx) != (0, 0) and (q, dy, dx) not in done:
                    tok_wait(q, (dy, dx))

        rows = tokens[dy * SIDE : (dy + 1) * SIDE].reshape(SIDE * span, tokens.shape[2])
        for weights, first in ((w_project, 0), (w_rest, project_width)):
            for begin in range(0, weights.shape[1], 2 * SPAN):
                end = min(begin + 2 * SPAN, weights.shape[1])
                product = jnp.dot(
                    rows, weights[:, begin:end], preferred_element_type=jnp.float32
                ).astype(jnp.bfloat16)
                for dx in range(SIDE):
                    pre[span_of(at(dy, dx)), first + begin : first + end] = product[
                        dx * span : (dx + 1) * span
                    ]
        here = (y + dy) % SIDE

        @pl.when(here == SIDE - 1)
        def _():
            to_tail.start()

        def block_at(i, here=here, firsts=firsts):
            c = here * SIDE + 1 + i
            for n, f in enumerate(firsts):
                c = jnp.where(i == SIDE - 1 + n, ((y + f) % SIDE) * SIDE, c)
            return c

        last = len(firsts) == 2

        def work(i, carry, block_at=block_at, last=last):
            local(block_at(i))
            if not last:
                inside(block_at(i))
            return carry

        lax.fori_loop(0, SIDE - 1 + len(firsts), work, 0)

    def chain(c, carry):
        state, total = carry
        end = cums[c, SPAN - 1 :]
        logs[c] = jnp.broadcast_to(total, (8, SPAN))
        keep = jnp.exp(end)
        later = []
        for h in range(heads):
            later.append(keep[:, h : h + 1] * state[head_of(h)] + fresh[c, head_of(h)])
        fresh[c] = state
        return jnp.concatenate(later, axis=0), total + end

    state, total = lax.fori_loop(
        0, blocks, chain, (jnp.zeros((width, N), jnp.float32), jnp.zeros((1, SPAN), jnp.float32))
    )
    slices = CTX // 2
    deep = width // slices
    scans = (ctx % 2) == (z % 2)

    def scanner(k):
        return 2 * k + k % 2

    decay = jnp.exp(total)
    third = lax.broadcasted_iota(jnp.int32, (deep, N), 0)
    for h in range(heads):
        whole = jnp.broadcast_to(decay[:, h : h + 1], (deep, N))
        high = whole.astype(jnp.bfloat16).astype(jnp.float32)
        middle = (whole - high).astype(jnp.bfloat16).astype(jnp.float32)
        low = whole - high - middle
        packed = jnp.where(
            third == 0, high, jnp.where(third == 1, middle, jnp.where(third == 2, low, 0.0))
        ).astype(jnp.bfloat16)
        for k in range(h * P_SIZE // deep, (h + 1) * P_SIZE // deep):
            own_state[k, :deep] = state[k * deep : (k + 1) * deep].astype(jnp.bfloat16)
            own_state[k, deep:] = packed

    def send_state(turned, carry):
        k = (z + turned) % slices
        to = scanner(k)

        @pl.when(to != ctx)
        def _():
            remote(
                own_state.at[k], in_state.at[ctx], state_send, state_recv, {"ctx": to}
            ).start()

        return carry

    lax.fori_loop(0, slices, send_state, 0)

    @pl.when(scans)
    def _():
        in_state[ctx] = own_state[z]

    def rest_inside(i, carry):
        inside(block_at(i))
        return carry

    lax.fori_loop(0, SIDE + 1, rest_inside, 0)

    @pl.when(scans)
    def _():
        landed(in_state.at[pl.ds(0, CTX - 1)], state_recv)

        def join(c, running):
            back[c] = running.astype(jnp.bfloat16)

            @pl.when(c != ctx)
            def _():
                remote(back.at[c], prior.at[z], back_send, back_recv, {"ctx": c}).start()

            came = in_state[c].astype(jnp.float32)
            keep = came[deep : deep + 1] + came[deep + 1 : deep + 2] + came[deep + 2 : deep + 3]
            return running * keep + came[:deep]

        lax.fori_loop(0, CTX, join, jnp.zeros((deep, N), jnp.float32))
        prior[z] = back[ctx]
        landed(prior.at[pl.ds(0, slices - 1)], back_recv)

    @pl.when(jnp.logical_not(scans))
    def _():
        landed(prior, back_recv)

    before = prior[...].astype(jnp.float32).reshape(width, N)
    low_rows = lax.broadcasted_iota(jnp.int32, (2 * P_SIZE, N), 0) < P_SIZE

    def finish(turned, carry):
        c = (inner + 1 + turned) % INNER
        reach = jnp.exp(logs[c, :1])
        for h in range(0, heads, 2):
            carried = jnp.where(low_rows, reach[:, h : h + 1], reach[:, h + 1 : h + 2])
            entered = fresh[c, pair_of(h)] + carried * before[pair_of(h)]
            high = entered.astype(jnp.bfloat16)
            low = (entered - high.astype(jnp.float32)).astype(jnp.bfloat16)
            over = diag[c, :, pair_of(h)]
            for share in (high, low):
                none = jnp.zeros_like(share)
                over = over + lax.dot_general(
                    scaled_c[span_of(c), h * N : (h + 2) * N],
                    jnp.concatenate(
                        [jnp.where(low_rows, share, none), jnp.where(low_rows, none, share)], axis=1
                    ),
                    (((1,), (1,)), ((), ())),
                    preferred_element_type=jnp.float32,
                )
            gated[c, :, pair_of(h)] = (over * opened[c, :, pair_of(h)]).astype(jnp.bfloat16)

        @pl.when(c != inner)
        def _():
            remote(gated.at[c], got.at[inner], out_send, out_recv, {"inner": c}).start()

        return carry

    lax.fori_loop(0, INNER, finish, 0)
    got[inner] = gated[inner]

    landed(tokens.at[pl.ds(0, INNER - 1)], tok_send)
    landed(parts.at[pl.ds(0, INNER - 1)], part_send)
    landed(w_project.at[rows_of(ctx)], wp_swap.at[0])
    landed(w_rest.at[rows_of(ctx)], wr_swap.at[0])

    @pl.when(core == 0)
    def _():
        landed(w_project, wp_send)
        landed(w_rest, wr_send)

    @pl.when(core == 1)
    def _():
        fewer = pl.ds(0, (depth - 2) * 2 * rows_here)
        landed(w_project.at[fewer], wp_send)
        landed(w_rest.at[fewer], wr_send)

    to_tail.wait_send()

    @pl.when(scans)
    def _():
        landed(own_state.at[pl.ds(0, slices - 1)], state_send)
        landed(back.at[pl.ds(0, CTX - 1)], back_send)

    @pl.when(jnp.logical_not(scans))
    def _():
        landed(own_state, state_send)

    landed(gated.at[pl.ds(0, INNER - 1)], out_send)
    landed(got.at[pl.ds(0, INNER - 1)], out_recv)


def norm_kernel(got, gain_ref, out_ref):
    span, width = got.shape[1], got.shape[2]
    share = INNER // G
    for group in range(G):
        squares = jnp.zeros((span, width), jnp.float32)
        for i in range(share):
            part = got[group * share + i].astype(jnp.float32)
            squares = squares + part * part
        power = jnp.sum(squares, axis=1, keepdims=True) / (share * width)
        scale = lax.rsqrt(power + EPSILON)
        for i in range(share):
            lanes = slice((group * share + i) * width, (group * share + i + 1) * width)
            part = got[group * share + i].astype(jnp.float32)
            out_ref[:, lanes] = (part * scale * gain_ref[:, lanes]).astype(jnp.bfloat16)


def on_device(
    tokens,
    project_weight,
    state_weight,
    step_weight,
    mixer_taps,
    state_taps,
    step_bias,
    decay_log,
    norm_gain,
):
    heads = step_weight.shape[1]
    rows_here = project_weight.shape[0]
    span, model = tokens.shape
    width = heads * P_SIZE
    total = span * INNER
    blocks = total // SPAN
    slices = CTX // 2
    deep = width // slices
    rest = 2 * N + SPAN
    vmem = pltpu.VMEM
    dma = pltpu.SemaphoreType.DMA
    bf16, f32 = jnp.bfloat16, jnp.float32
    got = pl.pallas_call(
        functools.partial(mixer_kernel, heads),
        out_shape=jax.ShapeDtypeStruct((INNER, span, width), bf16),
        in_specs=[pl.BlockSpec(memory_space=vmem)] * 8,
        out_specs=pl.BlockSpec(memory_space=vmem),
        scratch_shapes=[
            vmem((INNER, span, model), bf16),
            vmem((rows_here * CTX, 2 * width), bf16),
            vmem((rows_here * CTX, rest), bf16),
            vmem((G, 2 * N // INNER, rows_here), bf16),
            vmem((INNER, 2 * N // INNER, rows_here), bf16),
            vmem((total, 2 * width + rest), bf16),
            vmem((8, width + 2 * N), f32),
            vmem((16, width + 2 * N), bf16),
            vmem((16, width + 2 * N), bf16),
            vmem((total, width + 2 * N), bf16),
            vmem((blocks, SPAN, SPAN), f32),
            vmem((blocks, SPAN, SPAN), f32),
            vmem((blocks, 8, SPAN), f32),
            vmem((blocks, width, N), f32),
            vmem((blocks, SPAN, width), f32),
            vmem((total, heads * N), bf16),
            vmem((blocks, SPAN, width), f32),
            vmem((slices, 2 * deep, N), bf16),
            vmem((CTX, 2 * deep, N), bf16),
            vmem((CTX, deep, N), bf16),
            vmem((slices, deep, N), bf16),
            vmem((INNER, SPAN, width), bf16),
            dma,
            dma((QUARTERS * INNER,)),
            dma((2,)),
            dma((2,)),
            dma,
            dma((CTX,)),
            dma,
            dma((CTX,)),
        ]
        + [dma] * 10,
        compiler_params=pltpu.CompilerParams(
            collective_id=0, has_side_effects=True, vmem_limit_bytes=VMEM_LIMIT
        ),
        name="mixer",
    )(
        tokens,
        project_weight,
        state_weight.transpose(1, 2, 0),
        step_weight.T,
        mixer_taps,
        state_taps,
        step_bias[None],
        decay_log[None],
    )
    return pl.pallas_call(
        norm_kernel,
        out_shape=jax.ShapeDtypeStruct((span, INNER * width), bf16),
        in_specs=[pl.BlockSpec(memory_space=vmem)] * 2,
        out_specs=pl.BlockSpec(memory_space=vmem),
        name="norm",
    )(got, norm_gain[None])


def solution(mesh):
    placed = (
        P(("ctx", "inner"), None),
        P("ctx", None, "inner"),
        P("ctx", None, "inner"),
        P("ctx", "inner"),
        P(None, "inner"),
        P(),
        P("inner"),
        P("inner"),
        P(),
    )
    return jax.shard_map(
        on_device, mesh=mesh, in_specs=placed, out_specs=P(("ctx", "inner"), None), check_vma=False
    )
```

```python
import functools

import jax
import jax.numpy as jnp
from jax import lax
from jax.experimental import pallas as pl
from jax.experimental.pallas import tpu as pltpu
from jax.sharding import PartitionSpec as P

H = 64
P_SIZE = 64
N = 128
G = 4
CONV = 4
SPAN = 128
EPSILON = 1e-05
MESH = pl.DeviceIdType.MESH
CTX = 32
INNER = 16
SIDE = 4
QUARTERS = 4
VMEM_LIMIT = 60 * 1024 * 1024


def remote(src, dst, send_sem, recv_sem, device):
    return pltpu.make_async_remote_copy(
        src_ref=src,
        dst_ref=dst,
        send_sem=send_sem,
        recv_sem=recv_sem,
        device_id=device,
        device_id_type=MESH,
    )


def landed(ref, sem):
    pltpu.make_async_copy(ref, ref, sem).wait()


def mixer_kernel(
    heads,
    tok_ref,
    project_ref,
    state_ref,
    step_ref,
    mixer_ref,
    maps_ref,
    bias_ref,
    decay_ref,
    got,
    tokens,
    w_project,
    w_rest,
    pieces,
    parts,
    pre,
    taps,
    lead,
    tail,
    active,
    cums,
    steps,
    logs,
    fresh,
    diag,
    scaled_c,
    opened,
    own_state,
    own_decay,
    in_state,
    in_decay,
    back,
    prior,
    gated,
    tok_send,
    tok_recv,
    wp_swap,
    wr_swap,
    wp_send,
    wp_recv,
    wr_send,
    wr_recv,
    part_send,
    part_recv,
    tail_send,
    tail_recv,
    state_send,
    state_recv,
    decay_send,
    decay_recv,
    back_send,
    back_recv,
    out_send,
    out_recv,
):
    ctx = lax.axis_index("ctx")
    inner = lax.axis_index("inner")
    y, x = inner // SIDE, inner % SIDE
    rows_here = project_ref.shape[0]
    group = inner // (INNER // G)
    width = heads * P_SIZE
    other = ctx + 1 - 2 * (ctx % 2)
    up, down = (ctx + 2) % CTX, (ctx + CTX - 2) % CTX

    def at(dy, dx):
        return ((y + dy) % SIDE) * SIDE + (x + dx) % SIDE

    core = ctx % 2
    z = ctx // 2
    depth = CTX // 2
    way = 1 - 2 * core
    onward = (ctx + CTX + 2 * way) % CTX

    barrier = pltpu.get_barrier_semaphore()

    def greet(step, carry):
        pl.semaphore_signal(
            barrier, inc=1, device_id={"inner": (inner + step) % INNER}, device_id_type=MESH
        )
        return carry

    lax.fori_loop(1, INNER, greet, 0)
    for peer in (up, down, other):
        pl.semaphore_signal(barrier, inc=1, device_id={"ctx": peer}, device_id_type=MESH)

    def one_hot(index, target):
        return jnp.where(index == target, 1.0, 0.0).astype(jnp.bfloat16)

    def rows_of(place):
        return pl.ds(pl.multiple_of(place * rows_here, rows_here), rows_here)

    w_project[rows_of(ctx), :width] = project_ref[:, 0, :]
    w_project[rows_of(ctx), width:] = project_ref[:, 1, :]
    own_cols = state_ref.shape[0] * state_ref.shape[1]
    piece = N // INNER
    row = lax.broadcasted_iota(jnp.int32, (own_cols, own_cols), 0)
    col = lax.broadcasted_iota(jnp.int32, (own_cols, own_cols), 1)
    held = (row // piece % 2) * (own_cols // 2) + (row % piece) * G + row // (2 * piece)
    sorted_cols = jnp.dot(
        one_hot(held, col),
        state_ref[...].reshape(own_cols, rows_here),
        preferred_element_type=jnp.float32,
    ).astype(jnp.bfloat16)
    pieces[...] = sorted_cols.reshape(G, 2 * piece, rows_here)
    parts[inner] = pieces[group]
    row = lax.broadcasted_iota(jnp.int32, (heads, SPAN), 0)
    col = lax.broadcasted_iota(jnp.int32, (heads, SPAN), 1)
    w_rest[rows_of(ctx), 2 * N :] = lax.dot_general(
        step_ref[...],
        one_hot(row, col),
        (((0,), (0,)), ((), ())),
        preferred_element_type=jnp.float32,
    ).astype(jnp.bfloat16)
    row = lax.broadcasted_iota(jnp.int32, (G * N, N), 0)
    col = lax.broadcasted_iota(jnp.int32, (G * N, N), 1)
    pick = jnp.where(row == col * G + group, 1.0, 0.0)
    taps[: CONV + 1, :width] = mixer_ref[...]
    for side in range(2):
        taps[: CONV + 1, width + side * N : width + (side + 1) * N] = jnp.dot(
            maps_ref[:, side, :],
            pick,
            precision=lax.Precision.HIGHEST,
            preferred_element_type=jnp.float32,
        )
    lanes = jnp.zeros((1, SPAN - heads), jnp.float32)
    bias = jnp.concatenate([bias_ref[...], lanes], axis=1)
    rate = jnp.concatenate([-jnp.exp(decay_ref[...]), lanes], axis=1)
    tokens[0] = tok_ref[...]
    row = lax.broadcasted_iota(jnp.int32, (2 * N, 2 * N), 0)
    col = lax.broadcasted_iota(jnp.int32, (2 * N, 2 * N), 1)
    goes = one_hot((row // piece % 2) * N + (row // (2 * piece)) * piece + row % piece, col)

    pl.semaphore_wait(barrier, INNER - 1 + 3)

    def swap(ref, sems):
        return remote(
            ref.at[rows_of(ctx)], ref.at[rows_of(ctx)], sems.at[0], sems.at[1], {"ctx": other}
        )

    def swapped(ref, sems):
        landed(ref.at[rows_of(other)], sems.at[1])

    def w_copy(ref, place, to, send, recv):
        return remote(ref.at[rows_of(place)], ref.at[rows_of(place)], send, recv.at[place], {"ctx": to})

    def wp_copy(place, to):
        return w_copy(w_project, place, to, wp_send, wp_recv)

    def wr_copy(place, to):
        return w_copy(w_rest, place, to, wr_send, wr_recv)

    wp_copy(ctx, onward).start()
    swap(w_project, wp_swap).start()

    def send_part(step, carry):
        to = (inner + step) % INNER
        remote(
            pieces.at[to // (INNER // G)], parts.at[inner], part_send, part_recv, {"inner": to}
        ).start()
        return carry

    lax.fori_loop(1, INNER, send_part, 0)

    quarter = tok_ref.shape[0] // QUARTERS

    def tok_send_to(q, held, move):
        rows = pl.ds(q * quarter, quarter)
        (dy, dx), (ay, ax) = held, move
        slot = ((dy - ay) % SIDE) * SIDE + (dx - ax) % SIDE
        mine = (dy % SIDE) * SIDE + dx % SIDE
        source = tok_ref.at[rows] if mine == 0 else tokens.at[mine, rows]
        remote(
            source,
            tokens.at[slot, rows],
            tok_send,
            tok_recv.at[q * INNER + slot],
            {"inner": at(ay, ax)},
        ).start()

    def tok_wait(q, held):
        slot = (held[0] % SIDE) * SIDE + held[1] % SIDE
        landed(tokens.at[slot, pl.ds(q * quarter, quarter)], tok_recv.at[q * INNER + slot])

    def turn(q, along, across):
        return (across, along) if q < 2 else (along, across)

    def sense(q):
        return 1 if q % 2 == 0 else -1

    for q in range(QUARTERS):
        for d in (sense(q), -sense(q)):
            tok_send_to(q, (0, 0), turn(q, d, 0))
    swapped(w_project, wp_swap)
    wp_copy(other, onward).start()
    for q in range(QUARTERS):
        for d in (sense(q), -sense(q)):
            tok_send_to(q, (0, 0), turn(q, 0, d))

    landed(parts.at[pl.ds(0, INNER - 1)], part_recv)
    w_rest[rows_of(ctx), : 2 * N] = lax.dot_general(
        parts[...].reshape(2 * N, rows_here),
        goes,
        (((0,), (0,)), ((), ())),
        preferred_element_type=jnp.float32,
    ).astype(jnp.bfloat16)
    wr_copy(ctx, onward).start()
    swap(w_rest, wr_swap).start()

    def relay(copy, recv, ref, hop):
        def step():
            chip = (z + depth - way * hop) % depth
            for place in (2 * chip + core, 2 * chip + 1 - core):
                landed(ref.at[rows_of(place)], recv.at[place])
                if hop < depth // 2 - 1:
                    copy(place, onward).start()
                elif hop == depth // 2 - 1:

                    @pl.when(core == 0)
                    def _():
                        copy(place, onward).start()

                copy(place, other).start()

        if hop < depth // 2:
            step()
        else:
            pl.when(core == 0)(step)

    def wp_relay(hop):
        relay(wp_copy, wp_recv, w_project, hop)

    def wr_relay(hop):
        relay(wr_copy, wr_recv, w_rest, hop)

    def w_relay(hop):
        wp_relay(hop)
        wr_relay(hop)

    def arrive(q, along, across):
        d = sense(q)
        held = turn(q, along, across)
        tok_wait(q, held)
        if across == 0:
            if along == -d:
                tok_send_to(q, held, turn(q, d, 0))
            for e in (d, -d):
                tok_send_to(q, held, turn(q, 0, e))
        elif across == -d:
            tok_send_to(q, held, turn(q, 0, d))

    for q in range(QUARTERS):
        arrive(q, -sense(q), 0)
    wp_relay(1)
    swapped(w_rest, wr_swap)
    wr_copy(other, onward).start()
    for q in range(QUARTERS):
        arrive(q, sense(q), 0)
    wr_relay(1)
    w_relay(2)
    for q in range(QUARTERS):
        arrive(q, 0, -sense(q))
    w_relay(3)
    for q in range(QUARTERS):
        arrive(q, 2, 0)
    w_relay(4)
    w_relay(5)
    for q in range(QUARTERS):
        arrive(q, -sense(q), -sense(q))
    w_relay(6)
    w_relay(7)
    for q in range(QUARTERS):
        arrive(q, sense(q), -sense(q))
    w_relay(8)
    for q in range(QUARTERS):
        arrive(q, 2, -sense(q))

    def handed(hop, carry):
        chip = (z + depth + way * hop) % depth
        for place in (2 * chip, 2 * chip + 1):
            landed(w_project.at[rows_of(place)], wp_recv.at[place])
            landed(w_rest.at[rows_of(place)], wr_recv.at[place])
        return carry

    lax.fori_loop(1, depth // 2, handed, 0)

    @pl.when(core == 1)
    def _():
        handed(depth // 2, 0)

    project_width = w_project.shape[1]
    span = tok_ref.shape[0]
    blocks = pre.shape[0] // SPAN
    conv_cols = slice(width, 2 * width + 2 * N)
    row = lax.broadcasted_iota(jnp.int32, (SPAN, SPAN), 0)
    col = lax.broadcasted_iota(jnp.int32, (SPAN, SPAN), 1)
    lower = col <= row
    ones = jnp.where(lower, 1.0, 0.0)
    to_tail = remote(
        pre.at[pl.ds(blocks * SPAN - 16, 16), pl.ds(width, width + 2 * N)],
        tail,
        tail_send,
        tail_recv,
        {"ctx": (ctx + 1) % CTX},
    )

    def span_of(c):
        return pl.ds(pl.multiple_of(c * SPAN, SPAN), SPAN)

    def head_of(h):
        return slice(h * P_SIZE, (h + 1) * P_SIZE)

    def pair_of(h):
        return slice(h * P_SIZE, (h + 2) * P_SIZE)

    def silu(v):
        return v / (1.0 + jnp.exp(-v))

    def local(c):
        @pl.when(c == 0)
        def _():
            to_tail.wait_recv()
            edge = tail[...]
            lead[...] = jnp.where(ctx > 0, edge, jnp.zeros_like(edge))

        @pl.when(c > 0)
        def _():
            begin = pl.multiple_of(jnp.maximum(c * SPAN - 16, 0), 16)
            lead[...] = pre[pl.ds(begin, 16), conv_cols]

        raw = pre[span_of(c), 2 * width + 2 * N :].astype(jnp.float32) + bias
        step = jnp.maximum(raw, 0.0) + jnp.log1p(jnp.exp(-jnp.abs(raw)))
        cum = jnp.dot(
            ones,
            step * rate,
            precision=lax.Precision.HIGHEST,
            preferred_element_type=jnp.float32,
        )
        cums[c] = cum
        steps[c] = step
        current = pre[span_of(c), conv_cols]
        extended = jnp.concatenate([lead[...], current], axis=0).astype(jnp.float32)
        mixed = jnp.broadcast_to(taps[CONV : CONV + 1], current.shape)
        for k in range(CONV):
            begin = 16 - (CONV - 1) + k
            mixed = mixed + taps[k : k + 1] * extended[begin : begin + SPAN]
        values = silu(mixed).astype(jnp.bfloat16)
        active[span_of(c)] = values
        to_end = jnp.exp(cum[SPAN - 1 :] - cum) * step
        xs = values[:, :width].astype(jnp.float32).T.astype(jnp.bfloat16)
        bs = values[:, width : width + N].astype(jnp.float32)
        for h in range(heads):
            weighted = (bs * to_end[:, h : h + 1]).astype(jnp.bfloat16)
            fresh[c, head_of(h)] = jnp.dot(
                xs[head_of(h)], weighted, preferred_element_type=jnp.float32
            )

    def inside(c):
        values = active[span_of(c)]
        cum, step = cums[c], steps[c]
        cum_rows, step_rows = cum.T, step.T
        scores = lax.dot_general(
            values[:, width + N :],
            values[:, width : width + N],
            (((1,), (1,)), ((), ())),
            preferred_element_type=jnp.float32,
        )
        cs = values[:, width + N :].astype(jnp.float32)
        begun = jnp.exp(cum)
        lane = lax.broadcasted_iota(jnp.int32, (SPAN, 2 * P_SIZE), 1)
        for h in range(0, heads, 2):
            mixes, sides = [], []
            xs = values[:, pair_of(h)]
            for side in range(2):
                at_h = h + side
                gap = jnp.where(lower, cum[:, at_h : at_h + 1] - cum_rows[at_h : at_h + 1], -jnp.inf)
                mix = scores * jnp.exp(gap) * step_rows[at_h : at_h + 1]
                mixes.append(mix.astype(jnp.bfloat16))
                sides.append(jnp.where((lane < P_SIZE) == (side == 0), xs, jnp.zeros_like(xs)))
                scaled_c[span_of(c), at_h * N : (at_h + 1) * N] = (
                    cs * begun[:, at_h : at_h + 1]
                ).astype(jnp.bfloat16)
            diag[c, :, pair_of(h)] = jnp.dot(
                jnp.concatenate(mixes, axis=1),
                jnp.concatenate(sides, axis=0),
                preferred_element_type=jnp.float32,
            )
        opened[c] = silu(pre[span_of(c), :width].astype(jnp.float32))

    done = set()
    for q in range(QUARTERS):
        for along, across in ((-1, 0), (1, 0), (2, 0)):
            done.add((q,) + tuple(v % SIDE for v in turn(q, along, across)))
        for along in range(SIDE):
            done.add((q,) + tuple(v % SIDE for v in turn(q, along, -sense(q))))
    for dy, firsts in ((0, ()), (1, (1,)), (3, (0,)), (2, (2, 3))):
        for dx in range(SIDE):
            for q in range(QUARTERS):
                if (dy, dx) != (0, 0) and (q, dy, dx) not in done:
                    tok_wait(q, (dy, dx))

        rows = tokens[dy * SIDE : (dy + 1) * SIDE].reshape(SIDE * span, tokens.shape[2])
        for weights, first in ((w_project, 0), (w_rest, project_width)):
            for begin in range(0, weights.shape[1], 2 * SPAN):
                end = min(begin + 2 * SPAN, weights.shape[1])
                product = jnp.dot(
                    rows, weights[:, begin:end], preferred_element_type=jnp.float32
                ).astype(jnp.bfloat16)
                for dx in range(SIDE):
                    pre[span_of(at(dy, dx)), first + begin : first + end] = product[
                        dx * span : (dx + 1) * span
                    ]
        here = (y + dy) % SIDE

        @pl.when(here == SIDE - 1)
        def _():
            to_tail.start()

        def block_at(i, here=here, firsts=firsts):
            c = here * SIDE + 1 + i
            for n, f in enumerate(firsts):
                c = jnp.where(i == SIDE - 1 + n, ((y + f) % SIDE) * SIDE, c)
            return c

        def work(i, carry, block_at=block_at):
            local(block_at(i))
            return carry

        lax.fori_loop(0, SIDE - 1 + len(firsts), work, 0)

    def chain(c, carry):
        state, total = carry
        end = cums[c, SPAN - 1 :]
        logs[c] = jnp.broadcast_to(total, (8, SPAN))
        keep = jnp.exp(end)
        later = []
        for h in range(heads):
            later.append(keep[:, h : h + 1] * state[head_of(h)] + fresh[c, head_of(h)])
        fresh[c] = state
        return jnp.concatenate(later, axis=0), total + end

    state, total = lax.fori_loop(
        0, blocks, chain, (jnp.zeros((width, N), jnp.float32), jnp.zeros((1, SPAN), jnp.float32))
    )
    slices = CTX // 2
    deep = width // slices
    scans = (ctx % 2) == (z % 2)

    def scanner(k):
        return 2 * k + k % 2

    decay = jnp.exp(total)
    for h in range(heads):
        own_decay[h] = jnp.broadcast_to(decay[:, h : h + 1], (1, N))
    for k in range(slices):
        own_state[k] = state[k * deep : (k + 1) * deep].astype(jnp.bfloat16)

    def send_state(turned, carry):
        k = (z + turned) % slices
        to = scanner(k)

        @pl.when(to != ctx)
        def _():
            remote(
                own_decay.at[k * heads // slices],
                in_decay.at[ctx],
                decay_send,
                decay_recv,
                {"ctx": to},
            ).start()
            remote(
                own_state.at[k], in_state.at[ctx], state_send, state_recv, {"ctx": to}
            ).start()

        return carry

    lax.fori_loop(0, slices, send_state, 0)

    @pl.when(scans)
    def _():
        in_state[ctx] = own_state[z]
        in_decay[ctx] = own_decay[z * heads // slices]

    def all_inside(c, carry):
        inside(c)
        return carry

    early = blocks // 2
    lax.fori_loop(0, early, all_inside, 0)

    @pl.when(scans)
    def _():
        landed(in_decay.at[pl.ds(0, CTX - 1)], decay_recv)
        landed(in_state.at[pl.ds(0, CTX - 1)], state_recv)

        def join(c, running):
            back[c] = running.astype(jnp.bfloat16)

            @pl.when(c != ctx)
            def _():
                remote(back.at[c], prior.at[z], back_send, back_recv, {"ctx": c}).start()

            return running * in_decay[c] + in_state[c].astype(jnp.float32)

        lax.fori_loop(0, CTX, join, jnp.zeros((deep, N), jnp.float32))
        prior[z] = back[ctx]

    lax.fori_loop(early, blocks, all_inside, 0)

    @pl.when(scans)
    def _():
        landed(prior.at[pl.ds(0, slices - 1)], back_recv)

    @pl.when(jnp.logical_not(scans))
    def _():
        landed(prior, back_recv)

    before = prior[...].astype(jnp.float32).reshape(width, N)
    low_rows = lax.broadcasted_iota(jnp.int32, (2 * P_SIZE, N), 0) < P_SIZE

    def finish(turned, carry):
        c = (inner + 1 + turned) % INNER
        reach = jnp.exp(logs[c, :1])
        for h in range(0, heads, 2):
            carried = jnp.where(low_rows, reach[:, h : h + 1], reach[:, h + 1 : h + 2])
            entered = fresh[c, pair_of(h)] + carried * before[pair_of(h)]
            high = entered.astype(jnp.bfloat16)
            low = (entered - high.astype(jnp.float32)).astype(jnp.bfloat16)
            over = diag[c, :, pair_of(h)]
            for share in (high, low):
                none = jnp.zeros_like(share)
                over = over + lax.dot_general(
                    scaled_c[span_of(c), h * N : (h + 2) * N],
                    jnp.concatenate(
                        [jnp.where(low_rows, share, none), jnp.where(low_rows, none, share)], axis=1
                    ),
                    (((1,), (1,)), ((), ())),
                    preferred_element_type=jnp.float32,
                )
            gated[c, :, pair_of(h)] = (over * opened[c, :, pair_of(h)]).astype(jnp.bfloat16)

        @pl.when(c != inner)
        def _():
            remote(gated.at[c], got.at[inner], out_send, out_recv, {"inner": c}).start()

        return carry

    lax.fori_loop(0, INNER, finish, 0)
    got[inner] = gated[inner]

    landed(tokens.at[pl.ds(0, INNER - 1)], tok_send)
    landed(parts.at[pl.ds(0, INNER - 1)], part_send)
    landed(w_project.at[rows_of(ctx)], wp_swap.at[0])
    landed(w_rest.at[rows_of(ctx)], wr_swap.at[0])

    @pl.when(core == 0)
    def _():
        landed(w_project, wp_send)
        landed(w_rest, wr_send)

    @pl.when(core == 1)
    def _():
        fewer = pl.ds(0, (depth - 2) * 2 * rows_here)
        landed(w_project.at[fewer], wp_send)
        landed(w_rest.at[fewer], wr_send)

    to_tail.wait_send()

    @pl.when(scans)
    def _():
        landed(in_decay.at[pl.ds(0, slices - 1)], decay_send)
        landed(own_state.at[pl.ds(0, slices - 1)], state_send)
        landed(back.at[pl.ds(0, CTX - 1)], back_send)

    @pl.when(jnp.logical_not(scans))
    def _():
        landed(in_decay.at[pl.ds(0, slices)], decay_send)
        landed(own_state, state_send)

    landed(gated.at[pl.ds(0, INNER - 1)], out_send)
    landed(got.at[pl.ds(0, INNER - 1)], out_recv)


def norm_kernel(got, gain_ref, out_ref):
    span, width = got.shape[1], got.shape[2]
    share = INNER // G
    for group in range(G):
        squares = jnp.zeros((span, width), jnp.float32)
        for i in range(share):
            part = got[group * share + i].astype(jnp.float32)
            squares = squares + part * part
        power = jnp.sum(squares, axis=1, keepdims=True) / (share * width)
        scale = lax.rsqrt(power + EPSILON)
        for i in range(share):
            lanes = slice((group * share + i) * width, (group * share + i + 1) * width)
            part = got[group * share + i].astype(jnp.float32)
            out_ref[:, lanes] = (part * scale * gain_ref[:, lanes]).astype(jnp.bfloat16)


def on_device(
    tokens,
    project_weight,
    state_weight,
    step_weight,
    mixer_taps,
    state_taps,
    step_bias,
    decay_log,
    norm_gain,
):
    heads = step_weight.shape[1]
    rows_here = project_weight.shape[0]
    span, model = tokens.shape
    width = heads * P_SIZE
    total = span * INNER
    blocks = total // SPAN
    slices = CTX // 2
    deep = width // slices
    rest = 2 * N + SPAN
    vmem = pltpu.VMEM
    dma = pltpu.SemaphoreType.DMA
    bf16, f32 = jnp.bfloat16, jnp.float32
    got = pl.pallas_call(
        functools.partial(mixer_kernel, heads),
        out_shape=jax.ShapeDtypeStruct((INNER, span, width), bf16),
        in_specs=[pl.BlockSpec(memory_space=vmem)] * 8,
        out_specs=pl.BlockSpec(memory_space=vmem),
        scratch_shapes=[
            vmem((INNER, span, model), bf16),
            vmem((rows_here * CTX, 2 * width), bf16),
            vmem((rows_here * CTX, rest), bf16),
            vmem((G, 2 * N // INNER, rows_here), bf16),
            vmem((INNER, 2 * N // INNER, rows_here), bf16),
            vmem((total, 2 * width + rest), bf16),
            vmem((8, width + 2 * N), f32),
            vmem((16, width + 2 * N), bf16),
            vmem((16, width + 2 * N), bf16),
            vmem((total, width + 2 * N), bf16),
            vmem((blocks, SPAN, SPAN), f32),
            vmem((blocks, SPAN, SPAN), f32),
            vmem((blocks, 8, SPAN), f32),
            vmem((blocks, width, N), f32),
            vmem((blocks, SPAN, width), f32),
            vmem((total, heads * N), bf16),
            vmem((blocks, SPAN, width), f32),
            vmem((slices, deep, N), bf16),
            vmem((heads, 1, N), f32),
            vmem((CTX, deep, N), bf16),
            vmem((CTX, 1, N), f32),
            vmem((CTX, deep, N), bf16),
            vmem((slices, deep, N), bf16),
            vmem((INNER, SPAN, width), bf16),
            dma,
            dma((QUARTERS * INNER,)),
            dma((2,)),
            dma((2,)),
            dma,
            dma((CTX,)),
            dma,
            dma((CTX,)),
        ]
        + [dma] * 12,
        compiler_params=pltpu.CompilerParams(
            collective_id=0, has_side_effects=True, vmem_limit_bytes=VMEM_LIMIT
        ),
        name="mixer",
    )(
        tokens,
        project_weight,
        state_weight.transpose(1, 2, 0),
        step_weight.T,
        mixer_taps,
        state_taps,
        step_bias[None],
        decay_log[None],
    )
    return pl.pallas_call(
        norm_kernel,
        out_shape=jax.ShapeDtypeStruct((span, INNER * width), bf16),
        in_specs=[pl.BlockSpec(memory_space=vmem)] * 2,
        out_specs=pl.BlockSpec(memory_space=vmem),
        name="norm",
    )(got, norm_gain[None])


def solution(mesh):
    placed = (
        P(("ctx", "inner"), None),
        P("ctx", None, "inner"),
        P("ctx", None, "inner"),
        P("ctx", "inner"),
        P(None, "inner"),
        P(),
        P("inner"),
        P("inner"),
        P(),
    )
    return jax.shard_map(
        on_device, mesh=mesh, in_specs=placed, out_specs=P(("ctx", "inner"), None), check_vma=False
    )
```

```python
import functools

import jax
import jax.numpy as jnp
from jax import lax
from jax.experimental import pallas as pl
from jax.experimental.pallas import tpu as pltpu
from jax.sharding import PartitionSpec as P

H = 64
P_SIZE = 64
N = 128
G = 4
CONV = 4
SPAN = 128
EPSILON = 1e-05
MESH = pl.DeviceIdType.MESH
CTX = 32
INNER = 16
SIDE = 4
QUARTERS = 4
VMEM_LIMIT = 60 * 1024 * 1024


def remote(src, dst, send_sem, recv_sem, device):
    return pltpu.make_async_remote_copy(
        src_ref=src,
        dst_ref=dst,
        send_sem=send_sem,
        recv_sem=recv_sem,
        device_id=device,
        device_id_type=MESH,
    )


def landed(ref, sem):
    pltpu.make_async_copy(ref, ref, sem).wait()


def mixer_kernel(
    heads,
    tok_ref,
    project_ref,
    state_ref,
    step_ref,
    mixer_ref,
    maps_ref,
    bias_ref,
    decay_ref,
    got,
    tokens,
    w_project,
    w_rest,
    pieces,
    parts,
    pre,
    taps,
    lead,
    tail,
    active,
    cums,
    steps,
    logs,
    fresh,
    diag,
    scaled_c,
    opened,
    own_state,
    own_decay,
    in_state,
    in_decay,
    back,
    prior,
    gated,
    tok_send,
    tok_recv,
    wp_swap,
    wr_swap,
    wp_send,
    wp_recv,
    wr_send,
    wr_recv,
    part_send,
    part_recv,
    tail_send,
    tail_recv,
    state_send,
    state_recv,
    decay_send,
    decay_recv,
    back_send,
    back_recv,
    out_send,
    out_recv,
):
    ctx = lax.axis_index("ctx")
    inner = lax.axis_index("inner")
    y, x = inner // SIDE, inner % SIDE
    rows_here = project_ref.shape[0]
    group = inner // (INNER // G)
    width = heads * P_SIZE
    other = ctx + 1 - 2 * (ctx % 2)
    up, down = (ctx + 2) % CTX, (ctx + CTX - 2) % CTX

    def at(dy, dx):
        return ((y + dy) % SIDE) * SIDE + (x + dx) % SIDE

    core = ctx % 2
    z = ctx // 2
    depth = CTX // 2
    way = 1 - 2 * core
    onward = (ctx + CTX + 2 * way) % CTX

    barrier = pltpu.get_barrier_semaphore()

    def greet(step, carry):
        pl.semaphore_signal(
            barrier, inc=1, device_id={"inner": (inner + step) % INNER}, device_id_type=MESH
        )
        return carry

    lax.fori_loop(1, INNER, greet, 0)
    for peer in (up, down, other):
        pl.semaphore_signal(barrier, inc=1, device_id={"ctx": peer}, device_id_type=MESH)

    def one_hot(index, target):
        return jnp.where(index == target, 1.0, 0.0).astype(jnp.bfloat16)

    def rows_of(place):
        return pl.ds(pl.multiple_of(place * rows_here, rows_here), rows_here)

    w_project[rows_of(ctx), :width] = project_ref[:, 0, :]
    w_project[rows_of(ctx), width:] = project_ref[:, 1, :]
    own_cols = state_ref.shape[0] * state_ref.shape[1]
    piece = N // INNER
    row = lax.broadcasted_iota(jnp.int32, (own_cols, own_cols), 0)
    col = lax.broadcasted_iota(jnp.int32, (own_cols, own_cols), 1)
    held = (row // piece % 2) * (own_cols // 2) + (row % piece) * G + row // (2 * piece)
    sorted_cols = jnp.dot(
        one_hot(held, col),
        state_ref[...].reshape(own_cols, rows_here),
        preferred_element_type=jnp.float32,
    ).astype(jnp.bfloat16)
    pieces[...] = sorted_cols.reshape(G, 2 * piece, rows_here)
    parts[inner] = pieces[group]
    row = lax.broadcasted_iota(jnp.int32, (heads, SPAN), 0)
    col = lax.broadcasted_iota(jnp.int32, (heads, SPAN), 1)
    w_rest[rows_of(ctx), 2 * N :] = lax.dot_general(
        step_ref[...],
        one_hot(row, col),
        (((0,), (0,)), ((), ())),
        preferred_element_type=jnp.float32,
    ).astype(jnp.bfloat16)
    row = lax.broadcasted_iota(jnp.int32, (G * N, N), 0)
    col = lax.broadcasted_iota(jnp.int32, (G * N, N), 1)
    pick = jnp.where(row == col * G + group, 1.0, 0.0)
    taps[: CONV + 1, :width] = mixer_ref[...]
    for side in range(2):
        taps[: CONV + 1, width + side * N : width + (side + 1) * N] = jnp.dot(
            maps_ref[:, side, :],
            pick,
            precision=lax.Precision.HIGHEST,
            preferred_element_type=jnp.float32,
        )
    lanes = jnp.zeros((1, SPAN - heads), jnp.float32)
    bias = jnp.concatenate([bias_ref[...], lanes], axis=1)
    rate = jnp.concatenate([-jnp.exp(decay_ref[...]), lanes], axis=1)
    tokens[0] = tok_ref[...]
    row = lax.broadcasted_iota(jnp.int32, (2 * N, 2 * N), 0)
    col = lax.broadcasted_iota(jnp.int32, (2 * N, 2 * N), 1)
    goes = one_hot((row // piece % 2) * N + (row // (2 * piece)) * piece + row % piece, col)

    pl.semaphore_wait(barrier, INNER - 1 + 3)

    def swap(ref, sems):
        return remote(
            ref.at[rows_of(ctx)], ref.at[rows_of(ctx)], sems.at[0], sems.at[1], {"ctx": other}
        )

    def swapped(ref, sems):
        landed(ref.at[rows_of(other)], sems.at[1])

    def w_copy(ref, place, to, send, recv):
        return remote(ref.at[rows_of(place)], ref.at[rows_of(place)], send, recv.at[place], {"ctx": to})

    def wp_copy(place, to):
        return w_copy(w_project, place, to, wp_send, wp_recv)

    def wr_copy(place, to):
        return w_copy(w_rest, place, to, wr_send, wr_recv)

    wp_copy(ctx, onward).start()
    swap(w_project, wp_swap).start()

    def send_part(step, carry):
        to = (inner + step) % INNER
        remote(
            pieces.at[to // (INNER // G)], parts.at[inner], part_send, part_recv, {"inner": to}
        ).start()
        return carry

    lax.fori_loop(1, INNER, send_part, 0)

    quarter = tok_ref.shape[0] // QUARTERS

    def tok_send_to(q, held, move):
        rows = pl.ds(q * quarter, quarter)
        (dy, dx), (ay, ax) = held, move
        slot = ((dy - ay) % SIDE) * SIDE + (dx - ax) % SIDE
        mine = (dy % SIDE) * SIDE + dx % SIDE
        source = tok_ref.at[rows] if mine == 0 else tokens.at[mine, rows]
        remote(
            source,
            tokens.at[slot, rows],
            tok_send,
            tok_recv.at[q * INNER + slot],
            {"inner": at(ay, ax)},
        ).start()

    def tok_wait(q, held):
        slot = (held[0] % SIDE) * SIDE + held[1] % SIDE
        landed(tokens.at[slot, pl.ds(q * quarter, quarter)], tok_recv.at[q * INNER + slot])

    def turn(q, along, across):
        return (across, along) if q < 2 else (along, across)

    def sense(q):
        return 1 if q % 2 == 0 else -1

    for q in range(QUARTERS):
        for d in (sense(q), -sense(q)):
            tok_send_to(q, (0, 0), turn(q, d, 0))
    swapped(w_project, wp_swap)
    wp_copy(other, onward).start()
    for q in range(QUARTERS):
        for d in (sense(q), -sense(q)):
            tok_send_to(q, (0, 0), turn(q, 0, d))

    landed(parts.at[pl.ds(0, INNER - 1)], part_recv)
    w_rest[rows_of(ctx), : 2 * N] = lax.dot_general(
        parts[...].reshape(2 * N, rows_here),
        goes,
        (((0,), (0,)), ((), ())),
        preferred_element_type=jnp.float32,
    ).astype(jnp.bfloat16)
    wr_copy(ctx, onward).start()
    swap(w_rest, wr_swap).start()

    def relay(copy, recv, ref, hop):
        def step():
            chip = (z + depth - way * hop) % depth
            for place in (2 * chip + core, 2 * chip + 1 - core):
                landed(ref.at[rows_of(place)], recv.at[place])
                if hop < depth // 2 - 1:
                    copy(place, onward).start()
                elif hop == depth // 2 - 1:

                    @pl.when(core == 0)
                    def _():
                        copy(place, onward).start()

                copy(place, other).start()

        if hop < depth // 2:
            step()
        else:
            pl.when(core == 0)(step)

    def wp_relay(hop):
        relay(wp_copy, wp_recv, w_project, hop)

    def wr_relay(hop):
        relay(wr_copy, wr_recv, w_rest, hop)

    def w_relay(hop):
        wp_relay(hop)
        wr_relay(hop)

    def arrive(q, along, across):
        d = sense(q)
        held = turn(q, along, across)
        tok_wait(q, held)
        if across == 0:
            if along == -d:
                tok_send_to(q, held, turn(q, d, 0))
            for e in (d, -d):
                tok_send_to(q, held, turn(q, 0, e))
        elif across == -d:
            tok_send_to(q, held, turn(q, 0, d))

    for q in range(QUARTERS):
        arrive(q, -sense(q), 0)
    wp_relay(1)
    swapped(w_rest, wr_swap)
    wr_copy(other, onward).start()
    for q in range(QUARTERS):
        arrive(q, sense(q), 0)
    wr_relay(1)
    w_relay(2)
    for q in range(QUARTERS):
        arrive(q, 0, -sense(q))
    w_relay(3)
    for q in range(QUARTERS):
        arrive(q, 2, 0)
    w_relay(4)
    w_relay(5)
    for q in range(QUARTERS):
        arrive(q, -sense(q), -sense(q))
    w_relay(6)
    w_relay(7)
    for q in range(QUARTERS):
        arrive(q, sense(q), -sense(q))
    w_relay(8)
    for q in range(QUARTERS):
        arrive(q, 2, -sense(q))

    def handed(hop, carry):
        chip = (z + depth + way * hop) % depth
        for place in (2 * chip, 2 * chip + 1):
            landed(w_project.at[rows_of(place)], wp_recv.at[place])
            landed(w_rest.at[rows_of(place)], wr_recv.at[place])
        return carry

    lax.fori_loop(1, depth // 2, handed, 0)

    @pl.when(core == 1)
    def _():
        handed(depth // 2, 0)

    project_width = w_project.shape[1]
    span = tok_ref.shape[0]
    blocks = pre.shape[0] // SPAN
    conv_cols = slice(width, 2 * width + 2 * N)
    row = lax.broadcasted_iota(jnp.int32, (SPAN, SPAN), 0)
    col = lax.broadcasted_iota(jnp.int32, (SPAN, SPAN), 1)
    lower = col <= row
    ones = jnp.where(lower, 1.0, 0.0)
    to_tail = remote(
        pre.at[pl.ds(blocks * SPAN - 16, 16), pl.ds(width, width + 2 * N)],
        tail,
        tail_send,
        tail_recv,
        {"ctx": (ctx + 1) % CTX},
    )

    def span_of(c):
        return pl.ds(pl.multiple_of(c * SPAN, SPAN), SPAN)

    def head_of(h):
        return slice(h * P_SIZE, (h + 1) * P_SIZE)

    def pair_of(h):
        return slice(h * P_SIZE, (h + 2) * P_SIZE)

    def silu(v):
        return v / (1.0 + jnp.exp(-v))

    def local(c):
        @pl.when(c == 0)
        def _():
            to_tail.wait_recv()
            edge = tail[...]
            lead[...] = jnp.where(ctx > 0, edge, jnp.zeros_like(edge))

        @pl.when(c > 0)
        def _():
            begin = pl.multiple_of(jnp.maximum(c * SPAN - 16, 0), 16)
            lead[...] = pre[pl.ds(begin, 16), conv_cols]

        raw = pre[span_of(c), 2 * width + 2 * N :].astype(jnp.float32) + bias
        step = jnp.maximum(raw, 0.0) + jnp.log1p(jnp.exp(-jnp.abs(raw)))
        cum = jnp.dot(
            ones,
            step * rate,
            precision=lax.Precision.HIGHEST,
            preferred_element_type=jnp.float32,
        )
        cums[c] = cum
        steps[c] = step
        current = pre[span_of(c), conv_cols]
        extended = jnp.concatenate([lead[...], current], axis=0).astype(jnp.float32)
        mixed = jnp.broadcast_to(taps[CONV : CONV + 1], current.shape)
        for k in range(CONV):
            begin = 16 - (CONV - 1) + k
            mixed = mixed + taps[k : k + 1] * extended[begin : begin + SPAN]
        values = silu(mixed).astype(jnp.bfloat16)
        active[span_of(c)] = values
        to_end = jnp.exp(cum[SPAN - 1 :] - cum) * step
        xs = values[:, :width].astype(jnp.float32).T.astype(jnp.bfloat16)
        bs = values[:, width : width + N].astype(jnp.float32)
        for h in range(heads):
            weighted = (bs * to_end[:, h : h + 1]).astype(jnp.bfloat16)
            fresh[c, head_of(h)] = jnp.dot(
                xs[head_of(h)], weighted, preferred_element_type=jnp.float32
            )

    def inside(c):
        values = active[span_of(c)]
        cum, step = cums[c], steps[c]
        cum_rows, step_rows = cum.T, step.T
        scores = lax.dot_general(
            values[:, width + N :],
            values[:, width : width + N],
            (((1,), (1,)), ((), ())),
            preferred_element_type=jnp.float32,
        )
        cs = values[:, width + N :].astype(jnp.float32)
        begun = jnp.exp(cum)
        lane = lax.broadcasted_iota(jnp.int32, (SPAN, 2 * P_SIZE), 1)
        for h in range(0, heads, 2):
            mixes, sides = [], []
            xs = values[:, pair_of(h)]
            for side in range(2):
                at_h = h + side
                gap = jnp.where(lower, cum[:, at_h : at_h + 1] - cum_rows[at_h : at_h + 1], -jnp.inf)
                mix = scores * jnp.exp(gap) * step_rows[at_h : at_h + 1]
                mixes.append(mix.astype(jnp.bfloat16))
                sides.append(jnp.where((lane < P_SIZE) == (side == 0), xs, jnp.zeros_like(xs)))
                scaled_c[span_of(c), at_h * N : (at_h + 1) * N] = (
                    cs * begun[:, at_h : at_h + 1]
                ).astype(jnp.bfloat16)
            diag[c, :, pair_of(h)] = jnp.dot(
                jnp.concatenate(mixes, axis=1),
                jnp.concatenate(sides, axis=0),
                preferred_element_type=jnp.float32,
            )
        opened[c] = silu(pre[span_of(c), :width].astype(jnp.float32))

    done = set()
    for q in range(QUARTERS):
        for along, across in ((-1, 0), (1, 0), (2, 0)):
            done.add((q,) + tuple(v % SIDE for v in turn(q, along, across)))
        for along in range(SIDE):
            done.add((q,) + tuple(v % SIDE for v in turn(q, along, -sense(q))))
    for dy, firsts in ((0, ()), (1, (1,)), (3, (0,)), (2, (2, 3))):
        for dx in range(SIDE):
            for q in range(QUARTERS):
                if (dy, dx) != (0, 0) and (q, dy, dx) not in done:
                    tok_wait(q, (dy, dx))

        rows = tokens[dy * SIDE : (dy + 1) * SIDE].reshape(SIDE * span, tokens.shape[2])
        for weights, first in ((w_project, 0), (w_rest, project_width)):
            for begin in range(0, weights.shape[1], 2 * SPAN):
                end = min(begin + 2 * SPAN, weights.shape[1])
                product = jnp.dot(
                    rows, weights[:, begin:end], preferred_element_type=jnp.float32
                ).astype(jnp.bfloat16)
                for dx in range(SIDE):
                    pre[span_of(at(dy, dx)), first + begin : first + end] = product[
                        dx * span : (dx + 1) * span
                    ]
        here = (y + dy) % SIDE

        @pl.when(here == SIDE - 1)
        def _():
            to_tail.start()

        def block_at(i, here=here, firsts=firsts):
            c = here * SIDE + 1 + i
            for n, f in enumerate(firsts):
                c = jnp.where(i == SIDE - 1 + n, ((y + f) % SIDE) * SIDE, c)
            return c

        def work(i, carry, block_at=block_at):
            local(block_at(i))
            return carry

        lax.fori_loop(0, SIDE - 1 + len(firsts), work, 0)

    def chain(c, carry):
        state, total = carry
        end = cums[c, SPAN - 1 :]
        logs[c] = jnp.broadcast_to(total, (8, SPAN))
        keep = jnp.exp(end)
        later = []
        for h in range(heads):
            later.append(keep[:, h : h + 1] * state[head_of(h)] + fresh[c, head_of(h)])
        fresh[c] = state
        return jnp.concatenate(later, axis=0), total + end

    state, total = lax.fori_loop(
        0, blocks, chain, (jnp.zeros((width, N), jnp.float32), jnp.zeros((1, SPAN), jnp.float32))
    )
    slices = CTX // 2
    deep = width // slices
    scans = (ctx % 2) == (z % 2)

    def scanner(k):
        return 2 * k + k % 2

    decay = jnp.exp(total)
    for h in range(heads):
        own_decay[h] = jnp.broadcast_to(decay[:, h : h + 1], (1, N))
    for k in range(slices):
        own_state[k] = state[k * deep : (k + 1) * deep].astype(jnp.bfloat16)

    def send_state(turned, carry):
        k = (z + turned) % slices
        to = scanner(k)

        @pl.when(to != ctx)
        def _():
            remote(
                own_decay.at[k * heads // slices],
                in_decay.at[ctx],
                decay_send,
                decay_recv,
                {"ctx": to},
            ).start()
            remote(
                own_state.at[k], in_state.at[ctx], state_send, state_recv, {"ctx": to}
            ).start()

        return carry

    lax.fori_loop(0, slices, send_state, 0)

    @pl.when(scans)
    def _():
        in_state[ctx] = own_state[z]
        in_decay[ctx] = own_decay[z * heads // slices]

    def all_inside(c, carry):
        inside(c)
        return carry

    early = blocks // 2
    lax.fori_loop(0, early, all_inside, 0)

    @pl.when(scans)
    def _():
        landed(in_decay.at[pl.ds(0, CTX - 1)], decay_recv)
        landed(in_state.at[pl.ds(0, CTX - 1)], state_recv)

        def join(c, running):
            back[c] = running.astype(jnp.bfloat16)

            @pl.when(c != ctx)
            def _():
                remote(back.at[c], prior.at[z], back_send, back_recv, {"ctx": c}).start()

            return running * in_decay[c] + in_state[c].astype(jnp.float32)

        lax.fori_loop(0, CTX, join, jnp.zeros((deep, N), jnp.float32))
        prior[z] = back[ctx]

    lax.fori_loop(early, blocks, all_inside, 0)

    @pl.when(scans)
    def _():
        landed(prior.at[pl.ds(0, slices - 1)], back_recv)

    @pl.when(jnp.logical_not(scans))
    def _():
        landed(prior, back_recv)

    before = prior[...].astype(jnp.float32).reshape(width, N)
    low_rows = lax.broadcasted_iota(jnp.int32, (2 * P_SIZE, N), 0) < P_SIZE

    def finish(turned, carry):
        c = (inner + 1 + turned) % INNER
        reach = jnp.exp(logs[c, :1])
        for h in range(0, heads, 2):
            carried = jnp.where(low_rows, reach[:, h : h + 1], reach[:, h + 1 : h + 2])
            entered = fresh[c, pair_of(h)] + carried * before[pair_of(h)]
            high = entered.astype(jnp.bfloat16)
            low = (entered - high.astype(jnp.float32)).astype(jnp.bfloat16)
            over = diag[c, :, pair_of(h)]
            for share in (high, low):
                none = jnp.zeros_like(share)
                over = over + lax.dot_general(
                    scaled_c[span_of(c), h * N : (h + 2) * N],
                    jnp.concatenate(
                        [jnp.where(low_rows, share, none), jnp.where(low_rows, none, share)], axis=1
                    ),
                    (((1,), (1,)), ((), ())),
                    preferred_element_type=jnp.float32,
                )
            gated[c, :, pair_of(h)] = (over * opened[c, :, pair_of(h)]).astype(jnp.bfloat16)

        @pl.when(c != inner)
        def _():
            remote(gated.at[c], got.at[inner], out_send, out_recv, {"inner": c}).start()

        return carry

    lax.fori_loop(0, INNER, finish, 0)
    got[inner] = gated[inner]

    landed(tokens.at[pl.ds(0, INNER - 1)], tok_send)
    landed(parts.at[pl.ds(0, INNER - 1)], part_send)
    landed(w_project.at[rows_of(ctx)], wp_swap.at[0])
    landed(w_rest.at[rows_of(ctx)], wr_swap.at[0])

    @pl.when(core == 0)
    def _():
        landed(w_project, wp_send)
        landed(w_rest, wr_send)

    @pl.when(core == 1)
    def _():
        fewer = pl.ds(0, (depth - 2) * 2 * rows_here)
        landed(w_project.at[fewer], wp_send)
        landed(w_rest.at[fewer], wr_send)

    to_tail.wait_send()

    @pl.when(scans)
    def _():
        landed(in_decay.at[pl.ds(0, slices - 1)], decay_send)
        landed(own_state.at[pl.ds(0, slices - 1)], state_send)
        landed(back.at[pl.ds(0, CTX - 1)], back_send)

    @pl.when(jnp.logical_not(scans))
    def _():
        landed(in_decay.at[pl.ds(0, slices)], decay_send)
        landed(own_state, state_send)

    landed(gated.at[pl.ds(0, INNER - 1)], out_send)
    landed(got.at[pl.ds(0, INNER - 1)], out_recv)


def norm_kernel(got, gain_ref, out_ref):
    span, width = got.shape[1], got.shape[2]
    share = INNER // G
    for group in range(G):
        squares = jnp.zeros((span, width), jnp.float32)
        for i in range(share):
            part = got[group * share + i].astype(jnp.float32)
            squares = squares + part * part
        power = jnp.sum(squares, axis=1, keepdims=True) / (share * width)
        scale = lax.rsqrt(power + EPSILON)
        for i in range(share):
            lanes = slice((group * share + i) * width, (group * share + i + 1) * width)
            part = got[group * share + i].astype(jnp.float32)
            out_ref[:, lanes] = (part * scale * gain_ref[:, lanes]).astype(jnp.bfloat16)


def on_device(
    tokens,
    project_weight,
    state_weight,
    step_weight,
    mixer_taps,
    state_taps,
    step_bias,
    decay_log,
    norm_gain,
):
    heads = step_weight.shape[1]
    rows_here = project_weight.shape[0]
    span, model = tokens.shape
    width = heads * P_SIZE
    total = span * INNER
    blocks = total // SPAN
    slices = CTX // 2
    deep = width // slices
    rest = 2 * N + SPAN
    rows = span // 4
    vmem = pltpu.VMEM
    dma = pltpu.SemaphoreType.DMA
    bf16, f32 = jnp.bfloat16, jnp.float32
    got = pl.pallas_call(
        functools.partial(mixer_kernel, heads),
        out_shape=jax.ShapeDtypeStruct((INNER, span, width), bf16),
        in_specs=[pl.BlockSpec(memory_space=vmem)] * 8,
        out_specs=pl.BlockSpec(memory_space=vmem),
        scratch_shapes=[
            vmem((INNER, span, model), bf16),
            vmem((rows_here * CTX, 2 * width), bf16),
            vmem((rows_here * CTX, rest), bf16),
            vmem((G, 2 * N // INNER, rows_here), bf16),
            vmem((INNER, 2 * N // INNER, rows_here), bf16),
            vmem((total, 2 * width + rest), bf16),
            vmem((8, width + 2 * N), f32),
            vmem((16, width + 2 * N), bf16),
            vmem((16, width + 2 * N), bf16),
            vmem((total, width + 2 * N), bf16),
            vmem((blocks, SPAN, SPAN), f32),
            vmem((blocks, SPAN, SPAN), f32),
            vmem((blocks, 8, SPAN), f32),
            vmem((blocks, width, N), f32),
            vmem((blocks, SPAN, width), f32),
            vmem((total, heads * N), bf16),
            vmem((blocks, SPAN, width), f32),
            vmem((slices, deep, N), bf16),
            vmem((heads, 1, N), f32),
            vmem((CTX, deep, N), bf16),
            vmem((CTX, 1, N), f32),
            vmem((CTX, deep, N), bf16),
            vmem((slices, deep, N), bf16),
            vmem((INNER, SPAN, width), bf16),
            dma,
            dma((QUARTERS * INNER,)),
            dma((2,)),
            dma((2,)),
            dma,
            dma((CTX,)),
            dma,
            dma((CTX,)),
        ]
        + [dma] * 12,
        compiler_params=pltpu.CompilerParams(
            collective_id=0, has_side_effects=True, vmem_limit_bytes=VMEM_LIMIT
        ),
        name="mixer",
    )(
        tokens,
        project_weight,
        state_weight.transpose(1, 2, 0),
        step_weight.T,
        mixer_taps,
        state_taps,
        step_bias[None],
        decay_log[None],
    )
    return pl.pallas_call(
        norm_kernel,
        out_shape=jax.ShapeDtypeStruct((span, INNER * width), bf16),
        grid=(span // rows,),
        in_specs=[
            pl.BlockSpec((INNER, rows, width), lambda i: (0, i, 0)),
            pl.BlockSpec((1, INNER * width), lambda i: (0, 0)),
        ],
        out_specs=pl.BlockSpec((rows, INNER * width), lambda i: (i, 0)),
        name="norm",
    )(got, norm_gain[None])


def solution(mesh):
    placed = (
        P(("ctx", "inner"), None),
        P("ctx", None, "inner"),
        P("ctx", None, "inner"),
        P("ctx", "inner"),
        P(None, "inner"),
        P(),
        P("inner"),
        P("inner"),
        P(),
    )
    return jax.shard_map(
        on_device, mesh=mesh, in_specs=placed, out_specs=P(("ctx", "inner"), None), check_vma=False
    )
```
